512 devices in a mesh: dp: 64 (over x, z, core), seq: 8 (over y).
Axes of the slice: x: 4, y: 8, z: 8, core: 2. Of those that a mesh axis runs over, the one named last changes fastest.
Arguments:
- activations: bfloat16 [64, 1024, 1216], P('dp', 'seq'), may hold values from -6 to 6
- cotangent: bfloat16 [64, 1024, 2432], P('dp', 'seq'), may hold values from -0.5 to 0.5
- timesteps: int32 [64], P('dp'), may hold values from 0 to 15
- gate_table: float32 [16, 2432], replicated, may hold values from 0.1 to 1.9
- error_in: float32 [64, 1216, 2432], P('dp', 'seq'), may hold values from -6 to 6
- seed_factor: float32 [2432, 64], P('seq'), may hold values from -6 to 6
Outputs:
- error_out: float32 [64, 1216, 2432], P('dp', 'seq')
- column_factor: float32 [2432, 64], P('seq')
The draws below stay inside these ranges and needn't reach their ends.
All inputs are finite; a program needn't handle non-finite values.
Results may differ from the reference program's by a relative error of at most 0.00065.
Values may be sent and summed in bfloat16 or wider, within the bound.
A program may use at most 64 MiB of HBM per device.

```python
import jax
import jax.numpy as jnp
from jax import lax

DIN = 1216
DOUT = 2432
RANK = 64
STEPS = 16
TOK_DEV = 128
TOKENS = 1024
SAMPLES = 64
N_SEQ = 8


def plant(entries, stream_key, least, top_value):
    index_at = [jax.random.randint(jax.random.fold_in(stream_key, axis), (), 0, length) for axis, length in enumerate(entries.shape)]
    longest = entries.shape.index(max(entries.shape))
    beside = index_at[:longest] + [(index_at[longest] + 1) % entries.shape[longest]] + index_at[longest + 1:]
    return entries.at[tuple(index_at)].set(least).at[tuple(beside)].set(top_value)


def block_scale(stream_key, extent, pieces, smallest, largest):
    loudness = 1.0
    for position, shards_of in pieces:
        steps = jax.random.uniform(jax.random.fold_in(jax.random.fold_in(stream_key, 6), position), (shards_of,), jnp.float32, smallest / len(pieces), largest / len(pieces))
        loudness = loudness * jnp.repeat(jnp.exp(steps), extent[position] // shards_of).reshape((-1,) + (1,) * (len(extent) - 1 - position))
    return loudness


def scatter_about(rng, dims, width, most, shards=(), kind=jnp.bfloat16):
    drawn = width * jax.random.normal(rng, dims, jnp.float32)
    if shards:
        drawn = drawn * block_scale(rng, dims, shards, -0.22, 0.18)
    return jnp.clip(drawn, -most, most).astype(kind)


def setup_inputs(seed: int = 0) -> dict:
    seeds = jax.random.split(jax.random.key(seed), 7)
    activations = scatter_about(seeds[0], (SAMPLES, TOKENS, DIN), 1.0, 6.0, ((0, 64), (1, 8)))
    cotangent = scatter_about(seeds[1], (SAMPLES, TOKENS, DOUT), (1.0 / (TOK_DEV * N_SEQ) ** 0.5), 0.5, ((0, 64), (1, 8)))
    timesteps = plant(jax.random.randint(seeds[2], (SAMPLES,), 0, STEPS), jax.random.fold_in(seeds[2], 1), 0, STEPS - 1).astype(jnp.int32)
    gate_table = jnp.clip(1.0 + 0.18 * jax.random.normal(seeds[3], (STEPS, DOUT), jnp.float32), 0.1, 1.9)
    error_in = scatter_about(seeds[4], (SAMPLES, DIN, DOUT), 1.0, 6.0, ((0, 64), (1, 8)), jnp.float32)
    seed_factor = scatter_about(seeds[5], (DOUT, RANK), 1.0, 6.0, ((0, 8),), jnp.float32)
    return {"activations": activations, "cotangent": cotangent, "timesteps": timesteps, "gate_table": gate_table, "error_in": error_in, "seed_factor": seed_factor}


def reference(activations, cotangent, timesteps, gate_table, error_in, seed_factor):
    highest = lax.Precision.HIGHEST

    def per_sample(items):
        act_rows, cot_rows, step_index, memory = items
        gate_row = gate_table[step_index]
        gradient = jnp.dot(act_rows.T.astype(jnp.float32), cot_rows.astype(jnp.float32), preferred_element_type=jnp.float32) * gate_row
        merged = gradient + memory
        left = jnp.dot(merged, seed_factor, precision=highest)
        return (merged, left)
    merged_all, left_all = lax.map(per_sample, (activations, cotangent, timesteps, error_in))
    samples = activations.shape[0]
    left_mean = jnp.sum(left_all, 0) / samples
    gram = jnp.dot(left_mean.T, left_mean, precision=highest)
    chol = jnp.linalg.cholesky(gram)
    ortho = lax.linalg.triangular_solve(chol, left_mean, left_side=False, lower=True, transpose_a=True)

    def right_term(merged):
        return jnp.dot(merged.T, ortho, precision=highest)
    column_factor = jnp.sum(lax.map(right_term, merged_all), 0) / samples

    def new_memory(merged):
        return merged - jnp.dot(ortho, column_factor.T, precision=highest)
    error_out = lax.map(new_memory, merged_all)
    return (error_out, column_factor)
```

```python
import functools

import jax
import jax.numpy as jnp
from jax import lax
from jax.experimental import pallas as pl
from jax.experimental.pallas import tpu as pltpu
from jax.sharding import PartitionSpec as P

MESH = pl.DeviceIdType.MESH
F32 = jnp.float32
BF16 = jnp.bfloat16
NX, NZ, NC, NY = 4, 8, 2, 8
RANK = 64
DIN, DOUT = 1216, 2432
ROWS = DIN // NY
COLS = DOUT // NY
HALF = DIN // 2
SEED_PART = 160
SEED_SKIP = COLS - SEED_PART

LEFT_PLAN = (320, 80, 16)
RIGHT_PLAN = (608, 152, 24)


def split(value):
    high = value.astype(BF16)
    return high, (value - high.astype(F32)).astype(BF16)


def mm(first, second, dims=((1,), (0,))):
    return lax.dot_general(first, second, (dims, ((), ())), preferred_element_type=F32)


def place():
    replica = lax.axis_index("dp")
    return replica // (NZ * NC), (replica // NC) % NZ, replica % NC, lax.axis_index("seq")


def peers(axis):
    x, z, c, y = place()
    count = {"x": NX, "z": NZ, "core": NC, "y": NY}[axis]
    for step in range(1, count):
        if axis == "x":
            other = lax.rem(x + step, NX)
            yield other, (other * (NZ * NC) + z * NC + c, y)
        elif axis == "z":
            other = lax.rem(z + step, NZ)
            yield other, (x * (NZ * NC) + other * NC + c, y)
        elif axis == "core":
            other = 1 - c
            yield other, (x * (NZ * NC) + z * NC + other, y)
        else:
            other = lax.rem(y + step, NY)
            yield other, (x * (NZ * NC) + z * NC + c, other)


def exchange(axis, make, send_sems, recv_sems, during=None):
    copies = []
    for index, (other, device) in enumerate(peers(axis)):
        source, target = make(other)
        copy = pltpu.make_async_remote_copy(
            src_ref=source,
            dst_ref=target,
            send_sem=send_sems.at[index],
            recv_sem=recv_sems.at[index],
            device_id=device,
            device_id_type=MESH,
        )
        copy.start()
        copies.append(copy)
    if during is not None:
        during()
    for copy in copies:
        copy.wait()


def sum_everywhere(plan, local, bufs, sems, during):
    half_rows, x_rows, z_rows = plan
    from_core, half_sum, from_x, x_sum, from_z, z_sum, from_y, gather_z, total = bufs
    x, z, c, y = place()

    def sem(stage):
        return sems.at[0, stage], sems.at[1, stage]

    def part(index, rows):
        return pl.ds(pl.multiple_of(index * rows, 8), rows)

    exchange("core", lambda o: (local.at[part(o, half_rows)], from_core), *sem(0), during[0])
    half_sum[...] = local[part(c, half_rows), :] + from_core[...]

    exchange("x", lambda o: (half_sum.at[part(o, x_rows)], from_x.at[x]), *sem(1), during[1])
    from_x[x] = half_sum[part(x, x_rows), :]
    x_sum[0:x_rows, :] = (from_x[0] + from_x[1]) + (from_x[2] + from_x[3])

    exchange("z", lambda o: (x_sum.at[part(o, z_rows)], from_z.at[z]), *sem(2), during[2])
    from_z[z] = x_sum[part(z, z_rows), :]
    z_sum[...] = jnp.sum(from_z[...], axis=0)

    exchange("y", lambda o: (z_sum, from_y.at[y]), *sem(3), during[3])
    from_y[y] = z_sum[...]
    gather_z[z] = jnp.sum(from_y[...], axis=0)

    exchange("z", lambda o: (gather_z.at[z], gather_z.at[z]), *sem(4), during[4])
    total[part(c * NX + x, x_rows), :] = gather_z[...].reshape(NZ * z_rows, 128)[0:x_rows]

    mine = total.at[part(c * NX + x, x_rows)]
    exchange("x", lambda o: (mine, mine), *sem(5), during[5])

    mine_half = total.at[part(c, half_rows)]
    exchange("core", lambda o: (mine_half, mine_half), *sem(6), during[6])


def kernel(
    step_ref, table_ref, cot_ref, act_ref, mem_ref, seed_ref,
    ortho_ref, factor_ref,
    gate_ref, seed_mine, seed_other, seed_all, lhs, act4, left_rows, work, inverse,
    local1, core1, half1, x1, xs1, z1, zs1, y1, g1, total1,
    local2, core2, half2, x2, xs2, z2, zs2, y2, g2, total2,
    seed_sems, sems1, sems2,
):
    x, z, c, y = place()
    barrier = pltpu.get_barrier_semaphore()
    count = 0
    for axis in ("core", "x", "z", "y"):
        for _, device in peers(axis):
            pl.semaphore_signal(barrier, inc=1, device_id=device, device_id_type=MESH)
            count += 1
    pl.semaphore_wait(barrier, count)

    high, low = split(seed_ref[...])
    both = jnp.concatenate([high.astype(F32), low.astype(F32)], axis=0)
    packed = both.T.astype(BF16)
    seed_mine[y] = jnp.where(c == 0, packed[0:SEED_PART], packed[SEED_SKIP:COLS])

    def prepare():
        row = lax.broadcasted_iota(jnp.int32, table_ref.shape, 0)
        gate_ref[...] = jnp.sum(
            jnp.where(row == step_ref[0], table_ref[...], 0.0), axis=0, keepdims=True
        )
        gated_high, gated_low = split(cot_ref[...].astype(F32) * gate_ref[...])
        lhs[0:128, :] = gated_high
        lhs[128:256, :] = gated_low
        mem_high, mem_low = split(mem_ref[...])
        lhs[256 : 256 + ROWS, :] = mem_high
        lhs[416 : 416 + ROWS, :] = mem_low
        top, bottom = act_ref[0:HALF, :], act_ref[HALF:DIN, :]
        act4[:, 0:128] = top
        act4[:, 128:256] = top
        act4[:, 256:384] = bottom
        act4[:, 384:512] = bottom
        xs1[...] = jnp.zeros_like(xs1)
        xs2[...] = jnp.zeros_like(xs2)

    exchange(
        "y", lambda o: (seed_mine.at[y], seed_mine.at[y]),
        seed_sems.at[0, 0], seed_sems.at[1, 0], prepare,
    )
    exchange(
        "core", lambda o: (seed_mine, seed_other), seed_sems.at[0, 1], seed_sems.at[1, 1]
    )
    for block in range(NY):
        mine, other = seed_mine[block], seed_other[block]
        start = block * COLS
        seed_all[start : start + SEED_PART, :] = jnp.where(c == 0, mine, other)
        seed_all[start + SEED_PART : start + COLS, :] = jnp.where(
            c == 0, other, mine
        )[SEED_PART - SEED_SKIP : SEED_PART]

    product = mm(lhs[...], seed_all[...])
    tokens = product[0:128] + product[128:256]
    tokens = tokens[:, 0:RANK] + tokens[:, RANK:128]
    memory = product[256 : 256 + ROWS] + product[416 : 416 + ROWS]
    memory = memory[:, 0:RANK] + memory[:, RANK:128]
    tok_high, tok_low = split(tokens)
    column = jnp.concatenate([tok_high, tok_low], axis=0)
    blank = jnp.zeros_like(column)
    weights = jnp.concatenate(
        [
            jnp.concatenate([column, blank], axis=1),
            jnp.concatenate([blank, column], axis=1),
        ],
        axis=0,
    )
    local1[0:HALF, :] = mm(act4[...], weights)
    local1[HALF:640, :] = jnp.zeros((640 - HALF, 128), F32)
    my_rows = pl.ds(pl.multiple_of(lax.rem(y, 4) * ROWS, 8), ROWS)
    lane_half = lax.broadcasted_iota(jnp.int32, (ROWS, 128), 1) // RANK
    twice = jnp.concatenate([memory, memory], axis=1)
    local1[my_rows, :] = local1[my_rows, :] + jnp.where(lane_half == y // 4, twice, 0.0)

    sum_everywhere(
        LEFT_PLAN, local1, (core1, half1, x1, xs1, z1, zs1, y1, g1, total1), sems1, [None] * 7
    )

    left_high, left_low = split(total1[0:HALF, :])
    left_rows[0:HALF, :] = jnp.concatenate(
        [left_high[:, 0:RANK], left_low[:, 0:RANK]], axis=1
    )
    left_rows[HALF:DIN, :] = jnp.concatenate(
        [left_high[:, RANK:128], left_low[:, RANK:128]], axis=1
    )
    through = mm(left_rows[...], act_ref[...], ((0,), (0,)))
    through = through[0:RANK] + through[RANK:128]
    thr_high, thr_low = split(through)
    thr_both = jnp.concatenate([thr_high, thr_low], axis=0)
    pair = total1[my_rows, :]
    left_mine = jnp.where(y // 4 == 0, pair[:, 0:RANK], pair[:, RANK:128])
    mine_high, mine_low = split(left_mine)
    mine_both = jnp.concatenate([mine_high, mine_low], axis=1)
    for first, last in ((0, 4), (4, 8), (8, 12), (12, 16), (16, 19)):
        cols = slice(first * 128, last * 128)
        by_token = mm(thr_both, cot_ref[:, cols])
        by_high = mm(mine_both, lhs[256 : 256 + ROWS, cols], ((0,), (0,)))
        by_low = mm(mine_high, lhs[416 : 416 + ROWS, cols], ((0,), (0,)))
        right = (by_token[0:RANK] + by_token[RANK:128]) * gate_ref[:, cols]
        right = right + (by_high[0:RANK] + by_high[RANK:128]) + by_low
        for tile in range(first, last):
            at = (tile - first) * 128
            local2[tile * RANK : (tile + 1) * RANK, :] = right[:, at : at + 128]

    def gram():
        grams = mm(left_rows[...], left_rows[...], ((0,), (0,)))
        grams = grams[0:RANK] + grams[RANK:128]
        grams = grams[:, 0:RANK] + grams[:, RANK:128]
        row = lax.broadcasted_iota(jnp.int32, (RANK, RANK), 0)
        col = lax.broadcasted_iota(jnp.int32, (RANK, RANK), 1)
        work[...] = jnp.concatenate([grams, jnp.where(row == col, 1.0, 0.0)], axis=1)

    def eliminate(first, last):
        def step(k, carry):
            row = lax.broadcasted_iota(jnp.int32, (RANK, 128), 0)
            lane = lax.broadcasted_iota(jnp.int32, (RANK, 128), 1)
            whole = work[...]
            pivot_row = work[pl.ds(k, 1), :]
            column = jnp.sum(jnp.where(lane == k, whole, 0.0), axis=1, keepdims=True)
            pivot = jnp.sum(
                jnp.where(lane[0:1] == k, pivot_row, 0.0), axis=1, keepdims=True
            )
            ratio = jnp.where(row[:, 0:1] > k, column / pivot, 0.0)
            work[...] = whole - ratio * pivot_row
            return carry

        lax.fori_loop(first, last, step, 0)

    def finish():
        whole = work[...]
        row = lax.broadcasted_iota(jnp.int32, (RANK, 128), 0)
        lane = lax.broadcasted_iota(jnp.int32, (RANK, 128), 1)
        pivots = jnp.sum(jnp.where(row == lane, whole, 0.0), axis=1, keepdims=True)
        inverse[...] = whole[:, RANK:128] / jnp.sqrt(pivots)

    sum_everywhere(
        RIGHT_PLAN, local2, (core2, half2, x2, xs2, z2, zs2, y2, g2, total2), sems2,
        [
            gram,
            lambda: eliminate(0, 16),
            lambda: eliminate(16, 32),
            lambda: eliminate(32, 48),
            lambda: eliminate(48, 64),
            finish,
            None,
        ],
    )

    inv = inverse[...]
    inv_high, inv_low = split(inv)
    inv_lhs = jnp.concatenate(
        [inv_high.astype(F32), inv_high.astype(F32), inv_low.astype(F32)], axis=1
    ).astype(BF16)
    for tile in range(DOUT // 128):
        high, low = split(total2[tile * RANK : (tile + 1) * RANK, :])
        rhs = jnp.concatenate([high, low, high], axis=0)
        factor_ref[:, tile * 128 : (tile + 1) * 128] = mm(inv_lhs, rhs) * (1.0 / 64)
    ortho_ref[...] = lax.dot_general(
        left_mine, inv, (((1,), (1,)), ((), ())),
        precision=lax.Precision.HIGHEST, preferred_element_type=F32,
    )


def plan_scratch(plan):
    half_rows, x_rows, z_rows = plan
    return [
        pltpu.VMEM((2 * half_rows, 128), F32),
        pltpu.VMEM((half_rows, 128), F32),
        pltpu.VMEM((half_rows, 128), F32),
        pltpu.VMEM((NX, x_rows, 128), F32),
        pltpu.VMEM((NZ * z_rows, 128), F32),
        pltpu.VMEM((NZ, z_rows, 128), F32),
        pltpu.VMEM((z_rows, 128), F32),
        pltpu.VMEM((NY, z_rows, 128), F32),
        pltpu.VMEM((NZ, z_rows, 128), F32),
        pltpu.VMEM((2 * half_rows, 128), F32),
    ]


def factors(timesteps, gate_table, cot, act_t, memory, seed_t):
    vmem = pl.BlockSpec(memory_space=pltpu.VMEM)
    return pl.pallas_call(
        kernel,
        out_shape=(
            jax.ShapeDtypeStruct((ROWS, RANK), F32),
            jax.ShapeDtypeStruct((RANK, DOUT), F32),
        ),
        in_specs=[pl.BlockSpec(memory_space=pltpu.SMEM)] + [vmem] * 5,
        out_specs=(vmem, vmem),
        scratch_shapes=[
            pltpu.VMEM((1, DOUT), F32),
            pltpu.VMEM((NY, SEED_PART, 128), BF16),
            pltpu.VMEM((NY, SEED_PART, 128), BF16),
            pltpu.VMEM((DOUT, 128), BF16),
            pltpu.VMEM((576, DOUT), BF16),
            pltpu.VMEM((HALF, 512), BF16),
            pltpu.VMEM((DIN, 128), BF16),
            pltpu.VMEM((RANK, 128), F32),
            pltpu.VMEM((RANK, RANK), F32),
        ]
        + plan_scratch(LEFT_PLAN)
        + plan_scratch(RIGHT_PLAN)
        + [
            pltpu.SemaphoreType.DMA((2, 2, 7)),
            pltpu.SemaphoreType.DMA((2, 7, 7)),
            pltpu.SemaphoreType.DMA((2, 7, 7)),
        ],
        compiler_params=pltpu.CompilerParams(
            collective_id=0, has_side_effects=True, vmem_limit_bytes=48 * 2**20
        ),
    )(timesteps, gate_table, cot, act_t, memory, seed_t)


def per_device(activations, cotangent, timesteps, gate_table, error_in, seed_factor):
    act_rows = activations[0]
    cot_rows = cotangent[0]
    memory = error_in[0]
    step_ids = jnp.arange(gate_table.shape[0], dtype=jnp.int32)
    gate_row = jnp.sum(jnp.where(step_ids[:, None] == timesteps[0], gate_table, 0.0), 0)
    columns = lax.all_to_all(act_rows, "seq", split_axis=1, concat_axis=0, tiled=True)
    cot_all = lax.all_gather(cot_rows, "seq", axis=0, tiled=True)
    ortho, factor_t = factors(
        timesteps, gate_table, cot_rows, act_rows.T, memory, seed_factor.T
    )
    gradient = mm(columns, cot_all, ((0,), (0,)))
    merged = gradient * gate_row + memory
    error_out = merged - jnp.dot(ortho, factor_t, precision=lax.Precision.HIGHEST)
    factor_mine = lax.dynamic_slice_in_dim(
        factor_t, lax.axis_index("seq") * COLS, COLS, 1
    ).T
    return error_out[None], factor_mine


def solution(mesh):
    placed = (
        P("dp", "seq", None),
        P("dp", "seq", None),
        P("dp"),
        P(),
        P("dp", "seq", None),
        P("seq", None),
    )
    return jax.shard_map(
        per_device,
        mesh=mesh,
        in_specs=placed,
        out_specs=(P("dp", "seq", None), P("seq", None)),
        check_vma=False,
    )
```

```python
import functools

import jax
import jax.numpy as jnp
from jax import lax
from jax.experimental import pallas as pl
from jax.experimental.pallas import tpu as pltpu
from jax.sharding import PartitionSpec as P

MESH = pl.DeviceIdType.MESH
F32 = jnp.float32
BF16 = jnp.bfloat16
NX, NZ, NC, NY = 4, 8, 2, 8
RANK = 64
DIN, DOUT = 1216, 2432
ROWS = DIN // NY
COLS = DOUT // NY
HALF = DIN // 2
SEED_PART = 160
SEED_SKIP = COLS - SEED_PART

LEFT_PLAN = (320, 80, 16)
RIGHT_PLAN = (608, 152, 24)
CHUNKS = tuple(slice(at, min(at + 512, DOUT)) for at in range(0, DOUT, 512))


def split(value):
    high = value.astype(BF16)
    return high, (value - high.astype(F32)).astype(BF16)


def mm(first, second, dims=((1,), (0,))):
    return lax.dot_general(first, second, (dims, ((), ())), preferred_element_type=F32)


def place():
    replica = lax.axis_index("dp")
    return replica // (NZ * NC), (replica // NC) % NZ, replica % NC, lax.axis_index("seq")


def peers(axis):
    x, z, c, y = place()
    count = {"x": NX, "z": NZ, "core": NC, "y": NY}[axis]
    for step in range(1, count):
        if axis == "x":
            other = lax.rem(x + step, NX)
            yield other, (other * (NZ * NC) + z * NC + c, y)
        elif axis == "z":
            other = lax.rem(z + step, NZ)
            yield other, (x * (NZ * NC) + other * NC + c, y)
        elif axis == "core":
            other = 1 - c
            yield other, (x * (NZ * NC) + z * NC + other, y)
        else:
            other = lax.rem(y + step, NY)
            yield other, (x * (NZ * NC) + z * NC + c, other)


def start_exchange(axis, make, send_sems, recv_sems):
    copies = []
    for index, (other, device) in enumerate(peers(axis)):
        source, target = make(other)
        copy = pltpu.make_async_remote_copy(
            src_ref=source,
            dst_ref=target,
            send_sem=send_sems.at[index],
            recv_sem=recv_sems.at[index],
            device_id=device,
            device_id_type=MESH,
        )
        copy.start()
        copies.append(copy)
    return copies


def exchange(axis, make, send_sems, recv_sems, during=None):
    copies = start_exchange(axis, make, send_sems, recv_sems)
    if during is not None:
        during()
    for copy in copies:
        copy.wait()


class Ring:
    def __init__(self, blocks, sems):
        self.blocks, self.sems = blocks, sems
        x, z, c, y = place()
        self.y = y
        line = x * (NZ * NC) + z * NC + c
        self.device = ((line, lax.rem(y + 1, NY)), (line, lax.rem(y + NY - 1, NY)))
        self.sent = []

    def piece(self, way, steps_back, index):
        origin = self.y + (NY - steps_back if way == 0 else steps_back)
        half = index % 2 if way == 0 else 1 - index % 2
        return self.blocks.at[lax.rem(origin, NY), pl.ds(half * 64, 64)]

    def copy(self, way, index, piece):
        return pltpu.make_async_remote_copy(
            src_ref=piece,
            dst_ref=piece,
            send_sem=self.sems.at[0, way, index],
            recv_sem=self.sems.at[1, way, index],
            device_id=self.device[way],
            device_id_type=MESH,
        )

    def send(self, index):
        for way in range(2):
            copy = self.copy(way, index, self.piece(way, index // 2, index))
            copy.start()
            self.sent.append(copy)

    def receive(self, index):
        for way in range(2):
            self.copy(way, index, self.piece(way, index // 2 + 1, index)).wait_recv()

    def pass_on(self, index):
        self.receive(index)
        self.send(index + 2)

    def finish(self):
        for copy in self.sent:
            copy.wait_send()


def window(place_on_y):
    return pl.ds(pl.multiple_of(place_on_y * ROWS // 16 * 16, 16), SEED_PART)


def sum_everywhere(plan, local, bufs, sems, during):
    half_rows, x_rows, z_rows = plan
    from_core, half_sum, from_x, x_sum, from_z, z_sum, from_y, gather_z, total = bufs
    x, z, c, y = place()

    def sem(stage):
        return sems.at[0, stage], sems.at[1, stage]

    def part(index, rows):
        return pl.ds(pl.multiple_of(index * rows, 8), rows)

    exchange("core", lambda o: (local.at[part(o, half_rows)], from_core), *sem(0), during[0])
    half_sum[...] = local[part(c, half_rows), :] + from_core[...]

    exchange("x", lambda o: (half_sum.at[part(o, x_rows)], from_x.at[x]), *sem(1), during[1])
    from_x[x] = half_sum[part(x, x_rows), :]
    x_sum[0:x_rows, :] = (from_x[0] + from_x[1]) + (from_x[2] + from_x[3])

    exchange("z", lambda o: (x_sum.at[part(o, z_rows)], from_z.at[z]), *sem(2), during[2])
    from_z[z] = x_sum[part(z, z_rows), :]
    z_sum[...] = jnp.sum(from_z[...], axis=0)

    exchange("y", lambda o: (z_sum, from_y.at[y]), *sem(3), during[3])
    from_y[y] = z_sum[...]
    gather_z[z] = jnp.sum(from_y[...], axis=0)

    exchange("z", lambda o: (gather_z.at[z], gather_z.at[z]), *sem(4), during[4])
    total[part(c * NX + x, x_rows), :] = gather_z[...].reshape(NZ * z_rows, 128)[0:x_rows]

    mine = total.at[part(c * NX + x, x_rows)]
    exchange("x", lambda o: (mine, mine), *sem(5), during[5])

    mine_half = total.at[part(c, half_rows)]
    exchange("core", lambda o: (mine_half, mine_half), *sem(6), during[6])


def kernel(
    step_ref, table_ref, cot_hbm, act_hbm, mem_hbm, seed_ref,
    error_ref, factor_ref,
    cot_ref, act_ref, mem_ref, cot_all, act_all, act_mine,
    gate_ref, seed_mine, seed_other, seed_all, lhs, act4, left_rows, work, inverse, factor_all,
    local1, core1, half1, x1, xs1, z1, zs1, y1, g1, total1,
    local2, core2, half2, x2, xs2, z2, zs2, y2, g2, total2,
    load_sems, seed_sems, act_sems, ring_sems, sems1, sems2,
):
    x, z, c, y = place()
    barrier = pltpu.get_barrier_semaphore()
    count = 0
    for axis in ("core", "x", "z", "y"):
        for _, device in peers(axis):
            pl.semaphore_signal(barrier, inc=1, device_id=device, device_id_type=MESH)
            count += 1
    loads = [
        pltpu.make_async_copy(source, target, load_sems.at[index])
        for index, (source, target) in enumerate(
            ((cot_hbm, cot_ref), (act_hbm, act_ref), (mem_hbm, mem_ref))
        )
    ]
    for load in loads:
        load.start()
    ring = Ring(cot_all, ring_sems)

    high, low = split(seed_ref[...])
    both = jnp.concatenate([high.astype(F32), low.astype(F32)], axis=0)
    packed = both.T.astype(BF16)
    seed_mine[y] = jnp.where(c == 0, packed[0:SEED_PART], packed[SEED_SKIP:COLS])

    def prepare():
        for load in loads:
            load.wait()
        cot_all[y] = cot_ref[...]
        act_all[y] = act_ref[window(y), :]
        row = lax.broadcasted_iota(jnp.int32, table_ref.shape, 0)
        gate_ref[...] = jnp.sum(
            jnp.where(row == step_ref[0], table_ref[...], 0.0), axis=0, keepdims=True
        )
        gated_high, gated_low = split(cot_ref[...].astype(F32) * gate_ref[...])
        lhs[0:128, :] = gated_high
        lhs[128:256, :] = gated_low
        mem_high, mem_low = split(mem_ref[...])
        lhs[256 : 256 + ROWS, :] = mem_high
        lhs[416 : 416 + ROWS, :] = mem_low
        top, bottom = act_ref[0:HALF, :], act_ref[HALF:DIN, :]
        act4[:, 0:128] = top
        act4[:, 128:256] = top
        act4[:, 256:384] = bottom
        act4[:, 384:512] = bottom
        xs1[...] = jnp.zeros_like(xs1)
        xs2[...] = jnp.zeros_like(xs2)

    prepare()
    pl.semaphore_wait(barrier, count)
    exchange(
        "y", lambda o: (seed_mine.at[y], seed_mine.at[y]),
        seed_sems.at[0, 0], seed_sems.at[1, 0],
    )
    act_copies = []

    def first_blocks():
        act_copies.extend(
            start_exchange(
                "y", lambda o: (act_ref.at[window(o)], act_all.at[y]),
                act_sems.at[0], act_sems.at[1],
            )
        )
        ring.send(0)

    exchange(
        "core", lambda o: (seed_mine, seed_other), seed_sems.at[0, 1], seed_sems.at[1, 1],
        first_blocks,
    )
    for block in range(NY):
        mine, other = seed_mine[block], seed_other[block]
        start = block * COLS
        seed_all[start : start + SEED_PART, :] = jnp.where(c == 0, mine, other)
        seed_all[start + SEED_PART : start + COLS, :] = jnp.where(
            c == 0, other, mine
        )[SEED_PART - SEED_SKIP : SEED_PART]

    product = mm(lhs[...], seed_all[...])
    tokens = product[0:128] + product[128:256]
    tokens = tokens[:, 0:RANK] + tokens[:, RANK:128]
    memory = product[256 : 256 + ROWS] + product[416 : 416 + ROWS]
    memory = memory[:, 0:RANK] + memory[:, RANK:128]
    tok_high, tok_low = split(tokens)
    column = jnp.concatenate([tok_high, tok_low], axis=0)
    blank = jnp.zeros_like(column)
    weights = jnp.concatenate(
        [
            jnp.concatenate([column, blank], axis=1),
            jnp.concatenate([blank, column], axis=1),
        ],
        axis=0,
    )
    local1[0:HALF, :] = mm(act4[...], weights)
    local1[HALF:640, :] = jnp.zeros((640 - HALF, 128), F32)
    my_rows = pl.ds(pl.multiple_of(lax.rem(y, 4) * ROWS, 8), ROWS)
    lane_half = lax.broadcasted_iota(jnp.int32, (ROWS, 128), 1) // RANK
    twice = jnp.concatenate([memory, memory], axis=1)
    local1[my_rows, :] = local1[my_rows, :] + jnp.where(lane_half == y // 4, twice, 0.0)

    def later_blocks():
        ring.pass_on(0)
        ring.pass_on(1)

    sum_everywhere(
        LEFT_PLAN, local1, (core1, half1, x1, xs1, z1, zs1, y1, g1, total1), sems1,
        [None, lambda: ring.send(1), None, None, later_blocks, None, None],
    )

    left_high, left_low = split(total1[0:HALF, :])
    left_rows[0:HALF, :] = jnp.concatenate(
        [left_high[:, 0:RANK], left_low[:, 0:RANK]], axis=1
    )
    left_rows[HALF:DIN, :] = jnp.concatenate(
        [left_high[:, RANK:128], left_low[:, RANK:128]], axis=1
    )
    through = mm(left_rows[...], act_ref[...], ((0,), (0,)))
    through = through[0:RANK] + through[RANK:128]
    thr_high, thr_low = split(through)
    thr_both = jnp.concatenate([thr_high, thr_low], axis=0)
    pair = total1[my_rows, :]
    left_mine = jnp.where(y // 4 == 0, pair[:, 0:RANK], pair[:, RANK:128])
    mine_high, mine_low = split(left_mine)
    mine_both = jnp.concatenate([mine_high, mine_low], axis=1)
    for cols in CHUNKS:
        first, last = cols.start // 128, cols.stop // 128
        by_token = mm(thr_both, cot_ref[:, cols])
        by_high = mm(mine_both, lhs[256 : 256 + ROWS, cols], ((0,), (0,)))
        by_low = mm(mine_high, lhs[416 : 416 + ROWS, cols], ((0,), (0,)))
        right = (by_token[0:RANK] + by_token[RANK:128]) * gate_ref[:, cols]
        right = right + (by_high[0:RANK] + by_high[RANK:128]) + by_low
        for tile in range(first, last):
            at = (tile - first) * 128
            local2[tile * RANK : (tile + 1) * RANK, :] = right[:, at : at + 128]

    def gram():
        grams = mm(left_rows[...], left_rows[...], ((0,), (0,)))
        grams = grams[0:RANK] + grams[RANK:128]
        grams = grams[:, 0:RANK] + grams[:, RANK:128]
        row = lax.broadcasted_iota(jnp.int32, (RANK, RANK), 0)
        col = lax.broadcasted_iota(jnp.int32, (RANK, RANK), 1)
        work[...] = jnp.concatenate([grams, jnp.where(row == col, 1.0, 0.0)], axis=1)

    def eliminate(first, last):
        def step(k, carry):
            row = lax.broadcasted_iota(jnp.int32, (RANK, 128), 0)
            lane = lax.broadcasted_iota(jnp.int32, (RANK, 128), 1)
            whole = work[...]
            pivot_row = work[pl.ds(k, 1), :]
            column = jnp.sum(jnp.where(lane == k, whole, 0.0), axis=1, keepdims=True)
            pivot = jnp.sum(
                jnp.where(lane[0:1] == k, pivot_row, 0.0), axis=1, keepdims=True
            )
            ratio = jnp.where(row[:, 0:1] > k, column / pivot, 0.0)
            work[...] = whole - ratio * pivot_row
            return carry

        lax.fori_loop(first, last, step, 0)

    def finish():
        whole = work[...]
        row = lax.broadcasted_iota(jnp.int32, (RANK, 128), 0)
        lane = lax.broadcasted_iota(jnp.int32, (RANK, 128), 1)
        pivots = jnp.sum(jnp.where(row == lane, whole, 0.0), axis=1, keepdims=True)
        inverse[...] = whole[:, RANK:128] / jnp.sqrt(pivots)

    def merge():
        for source in range(NY):
            rows = act_all[source]
            act_mine[:, source * 128 : (source + 1) * 128] = jnp.where(
                lax.rem(y, 2) == 1, rows[8:SEED_PART], rows[0:ROWS]
            )
        for cols in CHUNKS:
            gradient = mm(act_mine[...], cot_all[:, :, cols].reshape(NY * 128, -1))
            error_ref[:, cols] = gradient * gate_ref[:, cols] + mem_ref[:, cols]

    def core_stage():
        ring.pass_on(2)
        ring.pass_on(3)
        gram()

    def z_stage():
        eliminate(16, 24)
        ring.pass_on(4)
        eliminate(24, 32)

    def gather_z_stage():
        eliminate(48, 64)
        finish()

    def gather_x_stage():
        ring.receive(5)
        ring.receive(6)
        for copy in act_copies:
            copy.wait()
        merge()

    sum_everywhere(
        RIGHT_PLAN, local2, (core2, half2, x2, xs2, z2, zs2, y2, g2, total2), sems2,
        [
            core_stage,
            lambda: eliminate(0, 16),
            z_stage,
            lambda: eliminate(32, 48),
            gather_z_stage,
            gather_x_stage,
            None,
        ],
    )

    inv = inverse[...]
    inv_high, inv_low = split(inv)
    inv_lhs = jnp.concatenate(
        [inv_high.astype(F32), inv_high.astype(F32), inv_low.astype(F32)], axis=1
    ).astype(BF16)
    ortho = lax.dot_general(
        left_mine, inv, (((1,), (1,)), ((), ())),
        precision=lax.Precision.HIGHEST, preferred_element_type=F32,
    )
    ort_high, ort_low = split(ortho)
    ortho_lhs = jnp.concatenate(
        [ort_high.astype(F32), ort_high.astype(F32), ort_low.astype(F32)], axis=1
    ).astype(BF16)
    for cols in CHUNKS:
        summed = jnp.concatenate(
            [
                total2[tile * RANK : (tile + 1) * RANK, :]
                for tile in range(cols.start // 128, cols.stop // 128)
            ],
            axis=1,
        )
        high, low = split(summed)
        factor = mm(inv_lhs, jnp.concatenate([high, low, high], axis=0)) * (1.0 / 64)
        factor_all[:, cols] = factor
        high, low = split(factor)
        error_ref[:, cols] = error_ref[:, cols] - mm(
            ortho_lhs, jnp.concatenate([high, low, high], axis=0)
        )
    mine = jnp.zeros((RANK, COLS), F32)
    for block in range(NY):
        part = factor_all[:, block * COLS : (block + 1) * COLS]
        mine = jnp.where(y == block, part, mine)
    factor_ref[...] = mine
    ring.finish()


def plan_scratch(plan):
    half_rows, x_rows, z_rows = plan
    return [
        pltpu.VMEM((2 * half_rows, 128), F32),
        pltpu.VMEM((half_rows, 128), F32),
        pltpu.VMEM((half_rows, 128), F32),
        pltpu.VMEM((NX, x_rows, 128), F32),
        pltpu.VMEM((NZ * z_rows, 128), F32),
        pltpu.VMEM((NZ, z_rows, 128), F32),
        pltpu.VMEM((z_rows, 128), F32),
        pltpu.VMEM((NY, z_rows, 128), F32),
        pltpu.VMEM((NZ, z_rows, 128), F32),
        pltpu.VMEM((2 * half_rows, 128), F32),
    ]


def factors(timesteps, gate_table, cot, act_t, memory, seed_t):
    vmem = pl.BlockSpec(memory_space=pltpu.VMEM)
    return pl.pallas_call(
        kernel,
        out_shape=(
            jax.ShapeDtypeStruct((ROWS, DOUT), F32),
            jax.ShapeDtypeStruct((RANK, COLS), F32),
        ),
        in_specs=[pl.BlockSpec(memory_space=pltpu.SMEM), vmem]
        + [pl.BlockSpec(memory_space=pl.ANY)] * 3
        + [vmem],
        out_specs=(vmem, vmem),
        scratch_shapes=[
            pltpu.VMEM((128, DOUT), BF16),
            pltpu.VMEM((DIN, 128), BF16),
            pltpu.VMEM((ROWS, DOUT), F32),
            pltpu.VMEM((NY, 128, DOUT), BF16),
            pltpu.VMEM((NY, SEED_PART, 128), BF16),
            pltpu.VMEM((ROWS, NY * 128), BF16),
            pltpu.VMEM((1, DOUT), F32),
            pltpu.VMEM((NY, SEED_PART, 128), BF16),
            pltpu.VMEM((NY, SEED_PART, 128), BF16),
            pltpu.VMEM((DOUT, 128), BF16),
            pltpu.VMEM((576, DOUT), BF16),
            pltpu.VMEM((HALF, 512), BF16),
            pltpu.VMEM((DIN, 128), BF16),
            pltpu.VMEM((RANK, 128), F32),
            pltpu.VMEM((RANK, RANK), F32),
            pltpu.VMEM((RANK, DOUT), F32),
        ]
        + plan_scratch(LEFT_PLAN)
        + plan_scratch(RIGHT_PLAN)
        + [
            pltpu.SemaphoreType.DMA((3,)),
            pltpu.SemaphoreType.DMA((2, 2, 7)),
            pltpu.SemaphoreType.DMA((2, 7)),
            pltpu.SemaphoreType.DMA((2, 2, 7)),
            pltpu.SemaphoreType.DMA((2, 7, 7)),
            pltpu.SemaphoreType.DMA((2, 7, 7)),
        ],
        compiler_params=pltpu.CompilerParams(
            collective_id=0, has_side_effects=True, vmem_limit_bytes=60 * 2**20
        ),
    )(timesteps, gate_table, cot, act_t, memory, seed_t)


def per_device(activations, cotangent, timesteps, gate_table, error_in, seed_factor):
    error_out, factor_t = factors(
        timesteps, gate_table, cotangent[0], activations[0].T, error_in[0], seed_factor.T
    )
    return error_out[None], factor_t.T


def solution(mesh):
    placed = (
        P("dp", "seq", None),
        P("dp", "seq", None),
        P("dp"),
        P(),
        P("dp", "seq", None),
        P("seq", None),
    )
    return jax.shard_map(
        per_device,
        mesh=mesh,
        in_specs=placed,
        out_specs=(P("dp", "seq", None), P("seq", None)),
        check_vma=False,
    )
```

```python
import functools

import jax
import jax.numpy as jnp
from jax import lax
from jax.experimental import pallas as pl
from jax.experimental.pallas import tpu as pltpu
from jax.sharding import PartitionSpec as P

MESH = pl.DeviceIdType.MESH
F32 = jnp.float32
BF16 = jnp.bfloat16
NX, NZ, NC, NY = 4, 8, 2, 8
RANK = 64
DIN, DOUT = 1216, 2432
ROWS = DIN // NY
COLS = DOUT // NY
HALF = DIN // 2
SEED_PART = 160
SEED_SKIP = COLS - SEED_PART

LEFT_PLAN = (320, 80, 16)
RIGHT_PLAN = (608, 152, 24)
CHUNKS = tuple(slice(at, min(at + 512, DOUT)) for at in range(0, DOUT, 512))


def split(value):
    high = value.astype(BF16)
    return high, (value - high.astype(F32)).astype(BF16)


def mm(first, second, dims=((1,), (0,))):
    return lax.dot_general(first, second, (dims, ((), ())), preferred_element_type=F32)


def place():
    replica = lax.axis_index("dp")
    return replica // (NZ * NC), (replica // NC) % NZ, replica % NC, lax.axis_index("seq")


def peers(axis):
    x, z, c, y = place()
    count = {"x": NX, "z": NZ, "core": NC, "y": NY}[axis]
    for step in range(1, count):
        if axis == "x":
            other = lax.rem(x + step, NX)
            yield other, (other * (NZ * NC) + z * NC + c, y)
        elif axis == "z":
            other = lax.rem(z + step, NZ)
            yield other, (x * (NZ * NC) + other * NC + c, y)
        elif axis == "core":
            other = 1 - c
            yield other, (x * (NZ * NC) + z * NC + other, y)
        else:
            other = lax.rem(y + step, NY)
            yield other, (x * (NZ * NC) + z * NC + c, other)


def start_exchange(axis, make, send_sems, recv_sems):
    copies = []
    for index, (other, device) in enumerate(peers(axis)):
        source, target = make(other)
        copy = pltpu.make_async_remote_copy(
            src_ref=source,
            dst_ref=target,
            send_sem=send_sems.at[index],
            recv_sem=recv_sems.at[index],
            device_id=device,
            device_id_type=MESH,
        )
        copy.start()
        copies.append(copy)
    return copies


def exchange(axis, make, send_sems, recv_sems, during=None):
    copies = start_exchange(axis, make, send_sems, recv_sems)
    if during is not None:
        during()
    for copy in copies:
        copy.wait()


class Ring:
    def __init__(self, blocks, sems):
        self.blocks, self.sems = blocks, sems
        x, z, c, y = place()
        self.y = y
        line = x * (NZ * NC) + z * NC + c
        self.device = ((line, lax.rem(y + 1, NY)), (line, lax.rem(y + NY - 1, NY)))
        self.sent = []

    def piece(self, way, steps_back, index):
        origin = self.y + (NY - steps_back if way == 0 else steps_back)
        half = index % 2 if way == 0 else 1 - index % 2
        return self.blocks.at[lax.rem(origin, NY), pl.ds(half * 64, 64)]

    def copy(self, way, index, piece):
        return pltpu.make_async_remote_copy(
            src_ref=piece,
            dst_ref=piece,
            send_sem=self.sems.at[0, way, index],
            recv_sem=self.sems.at[1, way, index],
            device_id=self.device[way],
            device_id_type=MESH,
        )

    def send(self, index):
        for way in range(2):
            copy = self.copy(way, index, self.piece(way, index // 2, index))
            copy.start()
            self.sent.append(copy)

    def receive(self, index):
        for way in range(2):
            self.copy(way, index, self.piece(way, index // 2 + 1, index)).wait_recv()

    def pass_on(self, index):
        self.receive(index)
        self.send(index + 2)

    def finish(self):
        for copy in self.sent:
            copy.wait_send()


def window(place_on_y):
    return pl.ds(pl.multiple_of(place_on_y * ROWS // 16 * 16, 16), SEED_PART)


def sum_everywhere(plan, local, bufs, sems, during):
    half_rows, x_rows, z_rows = plan
    from_core, half_sum, from_x, x_sum, from_z, z_sum, from_y, gather_z, total = bufs
    x, z, c, y = place()

    def sem(stage):
        return sems.at[0, stage], sems.at[1, stage]

    def part(index, rows):
        return pl.ds(pl.multiple_of(index * rows, 8), rows)

    exchange("core", lambda o: (local.at[part(o, half_rows)], from_core), *sem(0), during[0])
    half_sum[...] = local[part(c, half_rows), :] + from_core[...]

    exchange("x", lambda o: (half_sum.at[part(o, x_rows)], from_x.at[x]), *sem(1), during[1])
    from_x[x] = half_sum[part(x, x_rows), :]
    x_sum[0:x_rows, :] = (from_x[0] + from_x[1]) + (from_x[2] + from_x[3])

    exchange("z", lambda o: (x_sum.at[part(o, z_rows)], from_z.at[z]), *sem(2), during[2])
    from_z[z] = x_sum[part(z, z_rows), :]
    z_sum[...] = jnp.sum(from_z[...], axis=0)

    exchange("y", lambda o: (z_sum, from_y.at[y]), *sem(3), during[3])
    from_y[y] = z_sum[...]
    gather_z[z] = jnp.sum(from_y[...], axis=0)

    exchange("z", lambda o: (gather_z.at[z], gather_z.at[z]), *sem(4), during[4])
    total[part(c * NX + x, x_rows), :] = gather_z[...].reshape(NZ * z_rows, 128)[0:x_rows]

    mine = total.at[part(c * NX + x, x_rows)]
    exchange("x", lambda o: (mine, mine), *sem(5), during[5])

    mine_half = total.at[part(c, half_rows)]
    exchange("core", lambda o: (mine_half, mine_half), *sem(6), during[6])


def kernel(
    step_ref, table_ref, cot_hbm, act_hbm, mem_hbm, seed_ref,
    error_ref, factor_ref,
    cot_ref, act_ref, mem_ref, cot_all, act_all, act_mine,
    gate_ref, seed_mine, seed_other, seed_all, lhs, act4, left_rows, work, inverse, factor_all,
    local1, core1, half1, x1, xs1, z1, zs1, y1, g1, total1,
    local2, core2, half2, x2, xs2, z2, zs2, y2, g2, total2,
    load_sems, seed_sems, act_sems, ring_sems, sems1, sems2,
):
    x, z, c, y = place()
    barrier = pltpu.get_barrier_semaphore()
    count = 0
    for axis in ("core", "x", "z", "y"):
        for _, device in peers(axis):
            pl.semaphore_signal(barrier, inc=1, device_id=device, device_id_type=MESH)
            count += 1
    loads = [
        pltpu.make_async_copy(source, target, load_sems.at[index])
        for index, (source, target) in enumerate(
            ((cot_hbm, cot_ref), (act_hbm, act_ref), (mem_hbm, mem_ref))
        )
    ]
    for load in loads:
        load.start()
    ring = Ring(cot_all, ring_sems)

    high, low = split(seed_ref[...])
    both = jnp.concatenate([high.astype(F32), low.astype(F32)], axis=0)
    packed = both.T.astype(BF16)
    seed_mine[y] = jnp.where(c == 0, packed[0:SEED_PART], packed[SEED_SKIP:COLS])

    for load in loads:
        load.wait()
    cot_all[y] = cot_ref[...]
    act_all[y] = act_ref[window(y), :]
    act_copies = []

    def prepare():
        act_copies.extend(
            start_exchange(
                "y", lambda o: (act_ref.at[window(o)], act_all.at[y]),
                act_sems.at[0], act_sems.at[1],
            )
        )
        ring.send(0)
        row = lax.broadcasted_iota(jnp.int32, table_ref.shape, 0)
        gate_ref[...] = jnp.sum(
            jnp.where(row == step_ref[0], table_ref[...], 0.0), axis=0, keepdims=True
        )
        gated_high, gated_low = split(cot_ref[...].astype(F32) * gate_ref[...])
        lhs[0:128, :] = gated_high
        lhs[128:256, :] = gated_low
        mem_high, mem_low = split(mem_ref[...])
        lhs[256 : 256 + ROWS, :] = mem_high
        lhs[416 : 416 + ROWS, :] = mem_low
        top, bottom = act_ref[0:HALF, :], act_ref[HALF:DIN, :]
        act4[:, 0:128] = top
        act4[:, 128:256] = top
        act4[:, 256:384] = bottom
        act4[:, 384:512] = bottom
        xs1[...] = jnp.zeros_like(xs1)
        xs2[...] = jnp.zeros_like(xs2)

    pl.semaphore_wait(barrier, count)
    exchange(
        "y", lambda o: (seed_mine.at[y], seed_mine.at[y]),
        seed_sems.at[0, 0], seed_sems.at[1, 0], prepare,
    )
    exchange(
        "core", lambda o: (seed_mine, seed_other), seed_sems.at[0, 1], seed_sems.at[1, 1]
    )
    for block in range(NY):
        mine, other = seed_mine[block], seed_other[block]
        start = block * COLS
        seed_all[start : start + SEED_PART, :] = jnp.where(c == 0, mine, other)
        seed_all[start + SEED_PART : start + COLS, :] = jnp.where(
            c == 0, other, mine
        )[SEED_PART - SEED_SKIP : SEED_PART]

    product = mm(lhs[...], seed_all[...])
    tokens = product[0:128] + product[128:256]
    tokens = tokens[:, 0:RANK] + tokens[:, RANK:128]
    memory = product[256 : 256 + ROWS] + product[416 : 416 + ROWS]
    memory = memory[:, 0:RANK] + memory[:, RANK:128]
    tok_high, tok_low = split(tokens)
    column = jnp.concatenate([tok_high, tok_low], axis=0)
    blank = jnp.zeros_like(column)
    weights = jnp.concatenate(
        [
            jnp.concatenate([column, blank], axis=1),
            jnp.concatenate([blank, column], axis=1),
        ],
        axis=0,
    )
    local1[0:HALF, :] = mm(act4[...], weights)
    local1[HALF:640, :] = jnp.zeros((640 - HALF, 128), F32)
    my_rows = pl.ds(pl.multiple_of(lax.rem(y, 4) * ROWS, 8), ROWS)
    lane_half = lax.broadcasted_iota(jnp.int32, (ROWS, 128), 1) // RANK
    twice = jnp.concatenate([memory, memory], axis=1)
    local1[my_rows, :] = local1[my_rows, :] + jnp.where(lane_half == y // 4, twice, 0.0)

    def later_blocks():
        ring.send(1)
        ring.pass_on(0)

    sum_everywhere(
        LEFT_PLAN, local1, (core1, half1, x1, xs1, z1, zs1, y1, g1, total1), sems1,
        [None, None, None, None, later_blocks, lambda: ring.pass_on(1), None],
    )

    left_high, left_low = split(total1[0:HALF, :])
    left_rows[0:HALF, :] = jnp.concatenate(
        [left_high[:, 0:RANK], left_low[:, 0:RANK]], axis=1
    )
    left_rows[HALF:DIN, :] = jnp.concatenate(
        [left_high[:, RANK:128], left_low[:, RANK:128]], axis=1
    )
    through = mm(left_rows[...], act_ref[...], ((0,), (0,)))
    through = through[0:RANK] + through[RANK:128]
    thr_high, thr_low = split(through)
    thr_both = jnp.concatenate([thr_high, thr_low], axis=0)
    pair = total1[my_rows, :]
    left_mine = jnp.where(y // 4 == 0, pair[:, 0:RANK], pair[:, RANK:128])
    mine_high, mine_low = split(left_mine)
    mine_both = jnp.concatenate([mine_high, mine_low], axis=1)
    for cols in CHUNKS:
        first, last = cols.start // 128, cols.stop // 128
        by_token = mm(thr_both, cot_ref[:, cols])
        by_high = mm(mine_both, lhs[256 : 256 + ROWS, cols], ((0,), (0,)))
        by_low = mm(mine_high, lhs[416 : 416 + ROWS, cols], ((0,), (0,)))
        right = (by_token[0:RANK] + by_token[RANK:128]) * gate_ref[:, cols]
        right = right + (by_high[0:RANK] + by_high[RANK:128]) + by_low
        for tile in range(first, last):
            at = (tile - first) * 128
            local2[tile * RANK : (tile + 1) * RANK, :] = right[:, at : at + 128]

    def gram():
        grams = mm(left_rows[...], left_rows[...], ((0,), (0,)))
        grams = grams[0:RANK] + grams[RANK:128]
        grams = grams[:, 0:RANK] + grams[:, RANK:128]
        row = lax.broadcasted_iota(jnp.int32, (RANK, RANK), 0)
        col = lax.broadcasted_iota(jnp.int32, (RANK, RANK), 1)
        work[...] = jnp.concatenate([grams, jnp.where(row == col, 1.0, 0.0)], axis=1)

    def eliminate(first, last):
        def step(k, carry):
            row = lax.broadcasted_iota(jnp.int32, (RANK, 128), 0)
            lane = lax.broadcasted_iota(jnp.int32, (RANK, 128), 1)
            whole = work[...]
            pivot_row = work[pl.ds(k, 1), :]
            column = jnp.sum(jnp.where(lane == k, whole, 0.0), axis=1, keepdims=True)
            pivot = jnp.sum(
                jnp.where(lane[0:1] == k, pivot_row, 0.0), axis=1, keepdims=True
            )
            ratio = jnp.where(row[:, 0:1] > k, column / pivot, 0.0)
            work[...] = whole - ratio * pivot_row
            return carry

        lax.fori_loop(first, last, step, 0)

    def finish():
        whole = work[...]
        row = lax.broadcasted_iota(jnp.int32, (RANK, 128), 0)
        lane = lax.broadcasted_iota(jnp.int32, (RANK, 128), 1)
        pivots = jnp.sum(jnp.where(row == lane, whole, 0.0), axis=1, keepdims=True)
        inverse[...] = whole[:, RANK:128] / jnp.sqrt(pivots)

    def merge():
        for source in range(NY):
            rows = act_all[source]
            act_mine[:, source * 128 : (source + 1) * 128] = jnp.where(
                lax.rem(y, 2) == 1, rows[8:SEED_PART], rows[0:ROWS]
            )
        for cols in CHUNKS:
            gradient = mm(act_mine[...], cot_all[:, :, cols].reshape(NY * 128, -1))
            error_ref[:, cols] = gradient * gate_ref[:, cols] + mem_ref[:, cols]

    def core_stage():
        ring.pass_on(2)
        gram()

    def z_stage():
        eliminate(16, 32)

    def gather_z_stage():
        ring.pass_on(3)
        ring.pass_on(4)
        eliminate(48, 64)
        finish()

    def gather_x_stage():
        for copy in act_copies:
            copy.wait()

    sum_everywhere(
        RIGHT_PLAN, local2, (core2, half2, x2, xs2, z2, zs2, y2, g2, total2), sems2,
        [
            core_stage,
            lambda: eliminate(0, 16),
            z_stage,
            lambda: eliminate(32, 48),
            gather_z_stage,
            gather_x_stage,
            None,
        ],
    )

    ring.receive(5)
    ring.receive(6)
    merge()
    inv = inverse[...]
    inv_high, inv_low = split(inv)
    inv_lhs = jnp.concatenate(
        [inv_high.astype(F32), inv_high.astype(F32), inv_low.astype(F32)], axis=1
    ).astype(BF16)
    ortho = lax.dot_general(
        left_mine, inv, (((1,), (1,)), ((), ())),
        precision=lax.Precision.HIGHEST, preferred_element_type=F32,
    )
    ort_high, ort_low = split(ortho)
    ortho_lhs = jnp.concatenate(
        [ort_high.astype(F32), ort_high.astype(F32), ort_low.astype(F32)], axis=1
    ).astype(BF16)
    for cols in CHUNKS:
        summed = jnp.concatenate(
            [
                total2[tile * RANK : (tile + 1) * RANK, :]
                for tile in range(cols.start // 128, cols.stop // 128)
            ],
            axis=1,
        )
        high, low = split(summed)
        factor = mm(inv_lhs, jnp.concatenate([high, low, high], axis=0)) * (1.0 / 64)
        factor_all[:, cols] = factor
        high, low = split(factor)
        error_ref[:, cols] = error_ref[:, cols] - mm(
            ortho_lhs, jnp.concatenate([high, low, high], axis=0)
        )
    mine = jnp.zeros((RANK, COLS), F32)
    for block in range(NY):
        part = factor_all[:, block * COLS : (block + 1) * COLS]
        mine = jnp.where(y == block, part, mine)
    factor_ref[...] = mine
    ring.finish()


def plan_scratch(plan):
    half_rows, x_rows, z_rows = plan
    return [
        pltpu.VMEM((2 * half_rows, 128), F32),
        pltpu.VMEM((half_rows, 128), F32),
        pltpu.VMEM((half_rows, 128), F32),
        pltpu.VMEM((NX, x_rows, 128), F32),
        pltpu.VMEM((NZ * z_rows, 128), F32),
        pltpu.VMEM((NZ, z_rows, 128), F32),
        pltpu.VMEM((z_rows, 128), F32),
        pltpu.VMEM((NY, z_rows, 128), F32),
        pltpu.VMEM((NZ, z_rows, 128), F32),
        pltpu.VMEM((2 * half_rows, 128), F32),
    ]


def factors(timesteps, gate_table, cot, act_t, memory, seed_t):
    vmem = pl.BlockSpec(memory_space=pltpu.VMEM)
    return pl.pallas_call(
        kernel,
        out_shape=(
            jax.ShapeDtypeStruct((ROWS, DOUT), F32),
            jax.ShapeDtypeStruct((RANK, COLS), F32),
        ),
        in_specs=[pl.BlockSpec(memory_space=pltpu.SMEM), vmem]
        + [pl.BlockSpec(memory_space=pl.ANY)] * 3
        + [vmem],
        out_specs=(vmem, vmem),
        scratch_shapes=[
            pltpu.VMEM((128, DOUT), BF16),
            pltpu.VMEM((DIN, 128), BF16),
            pltpu.VMEM((ROWS, DOUT), F32),
            pltpu.VMEM((NY, 128, DOUT), BF16),
            pltpu.VMEM((NY, SEED_PART, 128), BF16),
            pltpu.VMEM((ROWS, NY * 128), BF16),
            pltpu.VMEM((1, DOUT), F32),
            pltpu.VMEM((NY, SEED_PART, 128), BF16),
            pltpu.VMEM((NY, SEED_PART, 128), BF16),
            pltpu.VMEM((DOUT, 128), BF16),
            pltpu.VMEM((576, DOUT), BF16),
            pltpu.VMEM((HALF, 512), BF16),
            pltpu.VMEM((DIN, 128), BF16),
            pltpu.VMEM((RANK, 128), F32),
            pltpu.VMEM((RANK, RANK), F32),
            pltpu.VMEM((RANK, DOUT), F32),
        ]
        + plan_scratch(LEFT_PLAN)
        + plan_scratch(RIGHT_PLAN)
        + [
            pltpu.SemaphoreType.DMA((3,)),
            pltpu.SemaphoreType.DMA((2, 2, 7)),
            pltpu.SemaphoreType.DMA((2, 7)),
            pltpu.SemaphoreType.DMA((2, 2, 7)),
            pltpu.SemaphoreType.DMA((2, 7, 7)),
            pltpu.SemaphoreType.DMA((2, 7, 7)),
        ],
        compiler_params=pltpu.CompilerParams(
            collective_id=0, has_side_effects=True, vmem_limit_bytes=60 * 2**20
        ),
    )(timesteps, gate_table, cot, act_t, memory, seed_t)


def per_device(activations, cotangent, timesteps, gate_table, error_in, seed_factor):
    error_out, factor_t = factors(
        timesteps, gate_table, cotangent[0], activations[0].T, error_in[0], seed_factor.T
    )
    return error_out[None], factor_t.T


def solution(mesh):
    placed = (
        P("dp", "seq", None),
        P("dp", "seq", None),
        P("dp"),
        P(),
        P("dp", "seq", None),
        P("seq", None),
    )
    return jax.shard_map(
        per_device,
        mesh=mesh,
        in_specs=placed,
        out_specs=(P("dp", "seq", None), P("seq", None)),
        check_vma=False,
    )
```

```python
import functools

import jax
import jax.numpy as jnp
from jax import lax
from jax.experimental import pallas as pl
from jax.experimental.pallas import tpu as pltpu
from jax.sharding import PartitionSpec as P

MESH = pl.DeviceIdType.MESH
F32 = jnp.float32
BF16 = jnp.bfloat16
NX, NZ, NC, NY = 4, 8, 2, 8
RANK = 64
DIN, DOUT = 1216, 2432
ROWS = DIN // NY
COLS = DOUT // NY
HALF = DIN // 2
SEED_PART = 160
SEED_SKIP = COLS - SEED_PART

LEFT_PLAN = (320, 80, 16)
RIGHT_PLAN = (608, 152, 24)
CHUNKS = tuple(slice(at, min(at + 512, DOUT)) for at in range(0, DOUT, 512))


def split(value):
    high = value.astype(BF16)
    return high, (value - high.astype(F32)).astype(BF16)


def mm(first, second, dims=((1,), (0,))):
    return lax.dot_general(first, second, (dims, ((), ())), preferred_element_type=F32)


def place():
    replica = lax.axis_index("dp")
    return replica // (NZ * NC), (replica // NC) % NZ, replica % NC, lax.axis_index("seq")


def peers(axis):
    x, z, c, y = place()
    count = {"x": NX, "z": NZ, "core": NC, "y": NY}[axis]
    for step in range(1, count):
        if axis == "x":
            other = lax.rem(x + step, NX)
            yield other, (other * (NZ * NC) + z * NC + c, y)
        elif axis == "z":
            other = lax.rem(z + step, NZ)
            yield other, (x * (NZ * NC) + other * NC + c, y)
        elif axis == "core":
            other = 1 - c
            yield other, (x * (NZ * NC) + z * NC + other, y)
        else:
            other = lax.rem(y + step, NY)
            yield other, (x * (NZ * NC) + z * NC + c, other)


def start_exchange(axis, make, send_sems, recv_sems):
    copies = []
    for index, (other, device) in enumerate(peers(axis)):
        source, target = make(other)
        copy = pltpu.make_async_remote_copy(
            src_ref=source,
            dst_ref=target,
            send_sem=send_sems.at[index],
            recv_sem=recv_sems.at[index],
            device_id=device,
            device_id_type=MESH,
        )
        copy.start()
        copies.append(copy)
    return copies


def exchange(axis, make, send_sems, recv_sems, during=None):
    copies = start_exchange(axis, make, send_sems, recv_sems)
    if during is not None:
        during()
    for copy in copies:
        copy.wait()


class Ring:
    def __init__(self, blocks, sems):
        self.blocks, self.sems = blocks, sems
        x, z, c, y = place()
        self.y = y
        line = x * (NZ * NC) + z * NC + c
        self.device = ((line, lax.rem(y + 1, NY)), (line, lax.rem(y + NY - 1, NY)))
        self.sent = []

    def piece(self, way, steps_back, index):
        origin = self.y + (NY - steps_back if way == 0 else steps_back)
        half = index % 2 if way == 0 else 1 - index % 2
        return self.blocks.at[lax.rem(origin, NY), pl.ds(half * 64, 64)]

    def copy(self, way, index, piece):
        return pltpu.make_async_remote_copy(
            src_ref=piece,
            dst_ref=piece,
            send_sem=self.sems.at[0, way, index],
            recv_sem=self.sems.at[1, way, index],
            device_id=self.device[way],
            device_id_type=MESH,
        )

    def send(self, index):
        for way in range(2):
            copy = self.copy(way, index, self.piece(way, index // 2, index))
            copy.start()
            self.sent.append(copy)

    def receive(self, index):
        for way in range(2):
            self.copy(way, index, self.piece(way, index // 2 + 1, index)).wait_recv()

    def pass_on(self, index):
        self.receive(index)
        self.send(index + 2)

    def finish(self):
        for copy in self.sent:
            copy.wait_send()


def window(place_on_y):
    return pl.ds(pl.multiple_of(place_on_y * ROWS // 16 * 16, 16), SEED_PART)


def sum_everywhere(plan, local, bufs, sems, during):
    half_rows, x_rows, z_rows = plan
    from_core, half_sum, from_x, x_sum, from_z, z_sum, from_y, gather_z, total = bufs
    x, z, c, y = place()

    def sem(stage):
        return sems.at[0, stage], sems.at[1, stage]

    def part(index, rows):
        return pl.ds(pl.multiple_of(index * rows, 8), rows)

    exchange("core", lambda o: (local.at[part(o, half_rows)], from_core), *sem(0), during[0])
    half_sum[...] = local[part(c, half_rows), :] + from_core[...]

    exchange("x", lambda o: (half_sum.at[part(o, x_rows)], from_x.at[x]), *sem(1), during[1])
    from_x[x] = half_sum[part(x, x_rows), :]
    x_sum[0:x_rows, :] = (from_x[0] + from_x[1]) + (from_x[2] + from_x[3])

    exchange("z", lambda o: (x_sum.at[part(o, z_rows)], from_z.at[z]), *sem(2), during[2])
    from_z[z] = x_sum[part(z, z_rows), :]
    z_sum[...] = jnp.sum(from_z[...], axis=0)

    exchange("y", lambda o: (z_sum, from_y.at[y]), *sem(3), during[3])
    from_y[y] = z_sum[...]
    gather_z[z] = jnp.sum(from_y[...], axis=0)

    exchange("z", lambda o: (gather_z.at[z], gather_z.at[z]), *sem(4), during[4])
    total[part(c * NX + x, x_rows), :] = gather_z[...].reshape(NZ * z_rows, 128)[0:x_rows]

    mine = total.at[part(c * NX + x, x_rows)]
    exchange("x", lambda o: (mine, mine), *sem(5), during[5])

    mine_half = total.at[part(c, half_rows)]
    exchange("core", lambda o: (mine_half, mine_half), *sem(6), during[6])


def kernel(
    step_ref, table_ref, cot_hbm, act_hbm, mem_hbm, seed_ref,
    error_ref, ortho_ref, parts_ref, factor_ref,
    cot_ref, act_ref, mem_ref, cot_all, act_all, act_mine,
    gate_ref, seed_mine, seed_other, seed_all, lhs, act4, left_rows, work, inverse, factor_all,
    local1, core1, half1, x1, xs1, z1, zs1, y1, g1, total1,
    local2, core2, half2, x2, xs2, z2, zs2, y2, g2, total2,
    load_sems, seed_sems, act_sems, ring_sems, sems1, sems2,
):
    x, z, c, y = place()
    barrier = pltpu.get_barrier_semaphore()
    count = 0
    for axis in ("core", "x", "z", "y"):
        for _, device in peers(axis):
            pl.semaphore_signal(barrier, inc=1, device_id=device, device_id_type=MESH)
            count += 1
    parts = [
        (source.at[pl.ds(at, step)], target.at[pl.ds(at, step)])
        for source, target, step in (
            (act_hbm, act_ref, 304), (cot_hbm, cot_ref, 32), (mem_hbm, mem_ref, 24),
        )
        for at in range(0, source.shape[0] // step * step, step)
    ]
    last = pl.ds(ROWS // 24 * 24, ROWS % 24)
    parts.append((mem_hbm.at[last], mem_ref.at[last]))
    loads = [
        pltpu.make_async_copy(source, target, load_sems.at[index])
        for index, (source, target) in enumerate(parts)
    ]
    for load in loads:
        load.start()
    ring = Ring(cot_all, ring_sems)

    high, low = split(seed_ref[...])
    both = jnp.concatenate([high.astype(F32), low.astype(F32)], axis=0)
    packed = both.T.astype(BF16)
    seed_mine[y] = jnp.where(c == 0, packed[0:SEED_PART], packed[SEED_SKIP:COLS])

    act_copies = []

    def prepare():
        for load in loads:
            load.wait()
        cot_all[y] = cot_ref[...]
        act_all[y] = act_ref[window(y), :]
        row = lax.broadcasted_iota(jnp.int32, table_ref.shape, 0)
        gate_ref[...] = jnp.sum(
            jnp.where(row == step_ref[0], table_ref[...], 0.0), axis=0, keepdims=True
        )
        gated_high, gated_low = split(cot_ref[...].astype(F32) * gate_ref[...])
        lhs[0:128, :] = gated_high
        lhs[128:256, :] = gated_low
        mem_high, mem_low = split(mem_ref[...])
        lhs[256 : 256 + ROWS, :] = mem_high
        lhs[416 : 416 + ROWS, :] = mem_low
        top, bottom = act_ref[0:HALF, :], act_ref[HALF:DIN, :]
        act4[:, 0:128] = top
        act4[:, 128:256] = top
        act4[:, 256:384] = bottom
        act4[:, 384:512] = bottom
        xs1[...] = jnp.zeros_like(xs1)
        xs2[...] = jnp.zeros_like(xs2)

    pl.semaphore_wait(barrier, count)
    def first_blocks():
        act_copies.extend(
            start_exchange(
                "y", lambda o: (act_ref.at[window(o)], act_all.at[y]),
                act_sems.at[0], act_sems.at[1],
            )
        )
        ring.send(0)

    def to_sibling(block, index):
        (_, device), = peers("core")
        copy = pltpu.make_async_remote_copy(
            src_ref=seed_mine.at[block],
            dst_ref=seed_other.at[block],
            send_sem=seed_sems.at[0, 1, index],
            recv_sem=seed_sems.at[1, 1, index],
            device_id=device,
            device_id_type=MESH,
        )
        copy.start()
        return copy

    along_y = start_exchange(
        "y", lambda o: (seed_mine.at[y], seed_mine.at[y]),
        seed_sems.at[0, 0], seed_sems.at[1, 0],
    )
    swaps = [to_sibling(y, 0)]
    prepare()
    for step in (1, 7, 2, 6, 3, 5, 4):
        along_y[step - 1].wait()
        swaps.append(to_sibling(lax.rem(y + NY - step, NY), step))
    first_blocks()
    for copy in swaps:
        copy.wait()
    for block in range(NY):
        mine, other = seed_mine[block], seed_other[block]
        start = block * COLS
        seed_all[start : start + SEED_PART, :] = jnp.where(c == 0, mine, other)
        seed_all[start + SEED_PART : start + COLS, :] = jnp.where(
            c == 0, other, mine
        )[SEED_PART - SEED_SKIP : SEED_PART]

    product = mm(lhs[...], seed_all[...])
    tokens = product[0:128] + product[128:256]
    tokens = tokens[:, 0:RANK] + tokens[:, RANK:128]
    memory = product[256 : 256 + ROWS] + product[416 : 416 + ROWS]
    memory = memory[:, 0:RANK] + memory[:, RANK:128]
    tok_high, tok_low = split(tokens)
    column = jnp.concatenate([tok_high, tok_low], axis=0)
    blank = jnp.zeros_like(column)
    weights = jnp.concatenate(
        [
            jnp.concatenate([column, blank], axis=1),
            jnp.concatenate([blank, column], axis=1),
        ],
        axis=0,
    )
    local1[0:HALF, :] = mm(act4[...], weights)
    local1[HALF:640, :] = jnp.zeros((640 - HALF, 128), F32)
    my_rows = pl.ds(pl.multiple_of(lax.rem(y, 4) * ROWS, 8), ROWS)
    lane_half = lax.broadcasted_iota(jnp.int32, (ROWS, 128), 1) // RANK
    twice = jnp.concatenate([memory, memory], axis=1)
    local1[my_rows, :] = local1[my_rows, :] + jnp.where(lane_half == y // 4, twice, 0.0)

    def later_blocks():
        ring.send(1)
        ring.pass_on(0)

    sum_everywhere(
        LEFT_PLAN, local1, (core1, half1, x1, xs1, z1, zs1, y1, g1, total1), sems1,
        [None, None, None, later_blocks, lambda: ring.pass_on(1), None, None],
    )

    left_high, left_low = split(total1[0:HALF, :])
    left_rows[0:HALF, :] = jnp.concatenate(
        [left_high[:, 0:RANK], left_low[:, 0:RANK]], axis=1
    )
    left_rows[HALF:DIN, :] = jnp.concatenate(
        [left_high[:, RANK:128], left_low[:, RANK:128]], axis=1
    )
    through = mm(left_rows[...], act_ref[...], ((0,), (0,)))
    through = through[0:RANK] + through[RANK:128]
    thr_high, thr_low = split(through)
    thr_both = jnp.concatenate([thr_high, thr_low], axis=0)
    pair = total1[my_rows, :]
    left_mine = jnp.where(y // 4 == 0, pair[:, 0:RANK], pair[:, RANK:128])
    mine_high, mine_low = split(left_mine)
    mine_both = jnp.concatenate([mine_high, mine_low], axis=1)
    for cols in CHUNKS:
        first, last = cols.start // 128, cols.stop // 128
        by_token = mm(thr_both, cot_ref[:, cols])
        by_high = mm(mine_both, lhs[256 : 256 + ROWS, cols], ((0,), (0,)))
        by_low = mm(mine_high, lhs[416 : 416 + ROWS, cols], ((0,), (0,)))
        right = (by_token[0:RANK] + by_token[RANK:128]) * gate_ref[:, cols]
        right = right + (by_high[0:RANK] + by_high[RANK:128]) + by_low
        for tile in range(first, last):
            at = (tile - first) * 128
            local2[tile * RANK : (tile + 1) * RANK, :] = right[:, at : at + 128]

    def gram():
        grams = mm(left_rows[...], left_rows[...], ((0,), (0,)))
        grams = grams[0:RANK] + grams[RANK:128]
        grams = grams[:, 0:RANK] + grams[:, RANK:128]
        row = lax.broadcasted_iota(jnp.int32, (RANK, RANK), 0)
        col = lax.broadcasted_iota(jnp.int32, (RANK, RANK), 1)
        work[...] = jnp.concatenate([grams, jnp.where(row == col, 1.0, 0.0)], axis=1)

    def eliminate(first, last):
        def step(k, carry):
            row = lax.broadcasted_iota(jnp.int32, (RANK, 128), 0)
            lane = lax.broadcasted_iota(jnp.int32, (RANK, 128), 1)
            whole = work[...]
            pivot_row = work[pl.ds(k, 1), :]
            column = jnp.sum(jnp.where(lane == k, whole, 0.0), axis=1, keepdims=True)
            pivot = jnp.sum(
                jnp.where(lane[0:1] == k, pivot_row, 0.0), axis=1, keepdims=True
            )
            ratio = jnp.where(row[:, 0:1] > k, column / pivot, 0.0)
            work[...] = whole - ratio * pivot_row
            return carry

        lax.fori_loop(first, last, step, 0)

    def finish():
        whole = work[...]
        row = lax.broadcasted_iota(jnp.int32, (RANK, 128), 0)
        lane = lax.broadcasted_iota(jnp.int32, (RANK, 128), 1)
        pivots = jnp.sum(jnp.where(row == lane, whole, 0.0), axis=1, keepdims=True)
        inverse[...] = whole[:, RANK:128] / jnp.sqrt(pivots)

    def merge():
        for source in range(NY):
            rows = act_all[source]
            act_mine[:, source * 128 : (source + 1) * 128] = jnp.where(
                lax.rem(y, 2) == 1, rows[8:SEED_PART], rows[0:ROWS]
            )
        for cols in CHUNKS:
            gradient = mm(act_mine[...], cot_all[:, :, cols].reshape(NY * 128, -1))
            error_ref[:, cols] = gradient * gate_ref[:, cols] + mem_ref[:, cols]

    def core_stage():
        ring.pass_on(2)
        gram()

    def y_stage():
        ring.pass_on(3)
        ring.pass_on(4)
        eliminate(32, 64)

    def gather_x_stage():
        for copy in act_copies:
            copy.wait()
        ring.receive(5)
        ring.receive(6)

    sum_everywhere(
        RIGHT_PLAN, local2, (core2, half2, x2, xs2, z2, zs2, y2, g2, total2), sems2,
        [
            core_stage,
            lambda: eliminate(0, 16),
            lambda: eliminate(16, 32),
            y_stage,
            finish,
            gather_x_stage,
            merge,
        ],
    )

    inv = inverse[...]
    inv_high, inv_low = split(inv)
    inv_lhs = jnp.concatenate(
        [inv_high.astype(F32), inv_high.astype(F32), inv_low.astype(F32)], axis=1
    ).astype(BF16)
    ortho = lax.dot_general(
        left_mine, inv, (((1,), (1,)), ((), ())),
        precision=lax.Precision.HIGHEST, preferred_element_type=F32,
    )
    ort_high, ort_low = split(ortho)
    ortho_ref[...] = jnp.concatenate(
        [ort_high.astype(F32), ort_high.astype(F32), ort_low.astype(F32)], axis=1
    ).astype(BF16)
    for cols in CHUNKS:
        summed = jnp.concatenate(
            [
                total2[tile * RANK : (tile + 1) * RANK, :]
                for tile in range(cols.start // 128, cols.stop // 128)
            ],
            axis=1,
        )
        high, low = split(summed)
        factor = mm(inv_lhs, jnp.concatenate([high, low, high], axis=0)) * (1.0 / 64)
        factor_all[:, cols] = factor
        high, low = split(factor)
        parts_ref[:, cols] = jnp.concatenate([high, low, high], axis=0)
    mine = jnp.zeros((RANK, COLS), F32)
    for block in range(NY):
        part = factor_all[:, block * COLS : (block + 1) * COLS]
        mine = jnp.where(y == block, part, mine)
    factor_ref[...] = mine
    ring.finish()


def plan_scratch(plan):
    half_rows, x_rows, z_rows = plan
    return [
        pltpu.VMEM((2 * half_rows, 128), F32),
        pltpu.VMEM((half_rows, 128), F32),
        pltpu.VMEM((half_rows, 128), F32),
        pltpu.VMEM((NX, x_rows, 128), F32),
        pltpu.VMEM((NZ * z_rows, 128), F32),
        pltpu.VMEM((NZ, z_rows, 128), F32),
        pltpu.VMEM((z_rows, 128), F32),
        pltpu.VMEM((NY, z_rows, 128), F32),
        pltpu.VMEM((NZ, z_rows, 128), F32),
        pltpu.VMEM((2 * half_rows, 128), F32),
    ]


def factors(timesteps, gate_table, cot, act_t, memory, seed_t):
    vmem = pl.BlockSpec(memory_space=pltpu.VMEM)
    return pl.pallas_call(
        kernel,
        out_shape=(
            pltpu.VMEM((ROWS, DOUT), F32),
            pltpu.VMEM((ROWS, 3 * RANK), BF16),
            pltpu.VMEM((3 * RANK, DOUT), BF16),
            pltpu.VMEM((RANK, COLS), F32),
        ),
        in_specs=[pl.BlockSpec(memory_space=pltpu.SMEM), vmem]
        + [pl.BlockSpec(memory_space=pltpu.HBM)] * 3
        + [vmem],
        out_specs=(vmem,) * 4,
        scratch_shapes=[
            pltpu.VMEM((128, DOUT), BF16),
            pltpu.VMEM((DIN, 128), BF16),
            pltpu.VMEM((ROWS, DOUT), F32),
            pltpu.VMEM((NY, 128, DOUT), BF16),
            pltpu.VMEM((NY, SEED_PART, 128), BF16),
            pltpu.VMEM((ROWS, NY * 128), BF16),
            pltpu.VMEM((1, DOUT), F32),
            pltpu.VMEM((NY, SEED_PART, 128), BF16),
            pltpu.VMEM((NY, SEED_PART, 128), BF16),
            pltpu.VMEM((DOUT, 128), BF16),
            pltpu.VMEM((576, DOUT), BF16),
            pltpu.VMEM((HALF, 512), BF16),
            pltpu.VMEM((DIN, 128), BF16),
            pltpu.VMEM((RANK, 128), F32),
            pltpu.VMEM((RANK, RANK), F32),
            pltpu.VMEM((RANK, DOUT), F32),
        ]
        + plan_scratch(LEFT_PLAN)
        + plan_scratch(RIGHT_PLAN)
        + [
            pltpu.SemaphoreType.DMA((16,)),
            pltpu.SemaphoreType.DMA((2, 2, 8)),
            pltpu.SemaphoreType.DMA((2, 7)),
            pltpu.SemaphoreType.DMA((2, 2, 7)),
            pltpu.SemaphoreType.DMA((2, 7, 7)),
            pltpu.SemaphoreType.DMA((2, 7, 7)),
        ],
        compiler_params=pltpu.CompilerParams(
            collective_id=0, has_side_effects=True, vmem_limit_bytes=60 * 2**20
        ),
    )(timesteps, gate_table, cot, act_t, memory, seed_t)


def store_kernel(
    merged_ref, ortho_ref, parts_ref, factor_ref, error_out, factor_out, error_ref, sems
):
    copies = [pltpu.make_async_copy(factor_ref, factor_out, sems.at[0])]
    copies[0].start()
    for index, cols in enumerate(CHUNKS):
        error_ref[:, cols] = merged_ref[:, cols] - mm(ortho_ref[...], parts_ref[:, cols])
        copies.append(
            pltpu.make_async_copy(
                error_ref.at[:, cols], error_out.at[:, cols], sems.at[index + 1]
            )
        )
        copies[-1].start()
    for copy in copies:
        copy.wait()


def store(merged, ortho, parts, factor):
    return pl.pallas_call(
        store_kernel,
        out_shape=(
            jax.ShapeDtypeStruct(merged.shape, F32),
            jax.ShapeDtypeStruct(factor.shape, F32),
        ),
        in_specs=[pl.BlockSpec(memory_space=pltpu.VMEM)] * 4,
        out_specs=(pl.BlockSpec(memory_space=pltpu.HBM),) * 2,
        scratch_shapes=[
            pltpu.VMEM((ROWS, DOUT), F32),
            pltpu.SemaphoreType.DMA((1 + len(CHUNKS),)),
        ],
        compiler_params=pltpu.CompilerParams(vmem_limit_bytes=16 * 2**20),
    )(merged, ortho, parts, factor)


def per_device(activations, cotangent, timesteps, gate_table, error_in, seed_factor):
    error_out, factor_t = store(
        *factors(
            timesteps, gate_table, cotangent[0], activations[0].T, error_in[0], seed_factor.T
        )
    )
    return error_out[None], factor_t.T


def solution(mesh):
    placed = (
        P("dp", "seq", None),
        P("dp", "seq", None),
        P("dp"),
        P(),
        P("dp", "seq", None),
        P("seq", None),
    )
    return jax.shard_map(
        per_device,
        mesh=mesh,
        in_specs=placed,
        out_specs=(P("dp", "seq", None), P("seq", None)),
        check_vma=False,
    )
```

```python
import functools

import jax
import jax.numpy as jnp
from jax import lax
from jax.experimental import pallas as pl
from jax.experimental.pallas import tpu as pltpu
from jax.sharding import PartitionSpec as P

MESH = pl.DeviceIdType.MESH
F32 = jnp.float32
BF16 = jnp.bfloat16
NX, NZ, NC, NY = 4, 8, 2, 8
RANK = 64
DIN, DOUT = 1216, 2432
ROWS = DIN // NY
COLS = DOUT // NY
HALF = DIN // 2
SEED_PART = 160
SEED_SKIP = COLS - SEED_PART

LEFT_PLAN = (320, 80, 16)
RIGHT_PLAN = (608, 152, 24)
CHUNKS = tuple(slice(at, min(at + 512, DOUT)) for at in range(0, DOUT, 512))


def split(value):
    high = value.astype(BF16)
    return high, (value - high.astype(F32)).astype(BF16)


def mm(first, second, dims=((1,), (0,))):
    return lax.dot_general(first, second, (dims, ((), ())), preferred_element_type=F32)


def place():
    replica = lax.axis_index("dp")
    return replica // (NZ * NC), (replica // NC) % NZ, replica % NC, lax.axis_index("seq")


def peers(axis):
    x, z, c, y = place()
    count = {"x": NX, "z": NZ, "core": NC, "y": NY}[axis]
    for step in range(1, count):
        if axis == "x":
            other = lax.rem(x + step, NX)
            yield other, (other * (NZ * NC) + z * NC + c, y)
        elif axis == "z":
            other = lax.rem(z + step, NZ)
            yield other, (x * (NZ * NC) + other * NC + c, y)
        elif axis == "core":
            other = 1 - c
            yield other, (x * (NZ * NC) + z * NC + other, y)
        else:
            other = lax.rem(y + step, NY)
            yield other, (x * (NZ * NC) + z * NC + c, other)


def start_exchange(axis, make, send_sems, recv_sems):
    copies = []
    for index, (other, device) in enumerate(peers(axis)):
        source, target = make(other)
        copy = pltpu.make_async_remote_copy(
            src_ref=source,
            dst_ref=target,
            send_sem=send_sems.at[index],
            recv_sem=recv_sems.at[index],
            device_id=device,
            device_id_type=MESH,
        )
        copy.start()
        copies.append(copy)
    return copies


def exchange(axis, make, send_sems, recv_sems, during=None):
    copies = start_exchange(axis, make, send_sems, recv_sems)
    if during is not None:
        during()
    for copy in copies:
        copy.wait()


class Ring:
    def __init__(self, blocks, sems):
        self.blocks, self.sems = blocks, sems
        x, z, c, y = place()
        self.y = y
        line = x * (NZ * NC) + z * NC + c
        self.device = ((line, lax.rem(y + 1, NY)), (line, lax.rem(y + NY - 1, NY)))
        self.sent = []

    def piece(self, way, steps_back, index):
        origin = self.y + (NY - steps_back if way == 0 else steps_back)
        half = index % 2 if way == 0 else 1 - index % 2
        return self.blocks.at[lax.rem(origin, NY), pl.ds(half * 64, 64)]

    def copy(self, way, index, piece):
        return pltpu.make_async_remote_copy(
            src_ref=piece,
            dst_ref=piece,
            send_sem=self.sems.at[0, way, index],
            recv_sem=self.sems.at[1, way, index],
            device_id=self.device[way],
            device_id_type=MESH,
        )

    def send(self, index):
        for way in range(2):
            copy = self.copy(way, index, self.piece(way, index // 2, index))
            copy.start()
            self.sent.append(copy)

    def receive(self, index):
        for way in range(2):
            self.copy(way, index, self.piece(way, index // 2 + 1, index)).wait_recv()

    def pass_on(self, index):
        self.receive(index)
        self.send(index + 2)

    def finish(self):
        for copy in self.sent:
            copy.wait_send()


def window(place_on_y):
    return pl.ds(pl.multiple_of(place_on_y * ROWS // 16 * 16, 16), SEED_PART)


def sum_everywhere(plan, local, bufs, sems, during):
    half_rows, x_rows, z_rows = plan
    used = -(-x_rows // z_rows)
    from_core, from_x, x_sum, from_z, z_sum, from_y, gathered, total = bufs
    x, z, c, y = place()
    (_, sibling), = peers("core")
    x_peers, z_peers = list(peers("x")), list(peers("z"))

    def part(index, rows):
        return pl.ds(pl.multiple_of(index * rows, 8), rows)

    def remote(stage, index, source, target, device):
        return pltpu.make_async_remote_copy(
            src_ref=source,
            dst_ref=target,
            send_sem=sems.at[0, stage, index],
            recv_sem=sems.at[1, stage, index],
            device_id=device,
            device_id_type=MESH,
        )

    def beside(stage):
        if during[stage] is not None:
            during[stage]()

    places = [other for other, _ in x_peers] + [x]
    copies = []
    for index, other in enumerate(places):
        mine = part((1 - c) * NX + other, x_rows)
        copies.append(
            remote(0, index, local.at[mine], from_core.at[part(other, x_rows)], sibling)
        )
        copies[-1].start()
    beside(0)
    x_copies = []
    for index, other in enumerate(places):
        copies[index].wait()
        rows = part(other, x_rows)
        both = local[part(c * NX + other, x_rows), :] + from_core[rows, :]
        if index < NX - 1:
            from_core[rows, :] = both
            x_copies.append(
                remote(1, index, from_core.at[rows], from_x.at[x], x_peers[index][1])
            )
            x_copies[-1].start()
        else:
            from_x[x] = both
    beside(1)
    for copy in x_copies:
        copy.wait()
    x_sum[0:x_rows, :] = (from_x[0] + from_x[1]) + (from_x[2] + from_x[3])

    copies = start_exchange(
        "z", lambda o: (x_sum.at[part(o, z_rows)], from_z.at[z]), sems.at[0, 2], sems.at[1, 2]
    )
    from_z[z] = x_sum[part(z, z_rows), :]
    beside(2)
    for copy in copies:
        copy.wait()
    z_sum[...] = jnp.sum(from_z[...], axis=0)

    copies = start_exchange("y", lambda o: (z_sum, from_y.at[y]), sems.at[0, 3], sems.at[1, 3])
    from_y[y] = z_sum[...]
    beside(3)
    for copy in copies:
        copy.wait()
    gathered[c, x, z] = jnp.sum(from_y[...], axis=0)

    def forward(step):
        piece = lax.rem(z + NZ - step, NZ)
        ref = gathered.at[c, x, piece]
        return piece < used, [
            remote(5 + index, piece, ref, ref, device)
            for index, (_, device) in enumerate(x_peers)
        ]

    def start_forward(step):
        wanted, forwards = forward(step)

        @pl.when(wanted)
        def _():
            for copy in forwards:
                copy.start()

    own = gathered.at[c, x, z]
    copies = start_exchange("z", lambda o: (own, own), sems.at[0, 4], sems.at[1, 4])
    start_forward(0)
    beside(4)
    for step in (1, 7, 2, 6, 3, 5, 4):
        copies[step - 1].wait()
        start_forward(step)

    def to_sibling(index, other):
        ref = gathered.at[c, other, pl.ds(0, used)]
        copy = remote(8, index, ref, ref, sibling)
        copy.start()
        return copy

    copies = [to_sibling(0, x)]
    beside(5)
    for index in (0, 2, 1):
        other = lax.rem(x + NX - 1 - index, NX)
        for piece in range(used):
            ref = gathered.at[c, other, piece]
            remote(5 + index, piece, ref, ref, x_peers[index][1]).wait_recv()
        copies.append(to_sibling(1 + index, other))
    beside(6)
    for copy in copies:
        copy.wait()
    for step in range(NZ):
        wanted, forwards = forward(step)

        @pl.when(wanted)
        def _():
            for copy in forwards:
                copy.wait_send()

    for core in range(NC):
        for at in range(NX):
            first = (core * NX + at) * x_rows
            total[first : first + x_rows, :] = (
                gathered[core, at].reshape(NZ * z_rows, 128)[0:x_rows]
            )


def kernel(
    step_ref, table_ref, cot_hbm, act_hbm, mem_hbm, seed_ref,
    error_ref, ortho_ref, parts_ref, factor_ref,
    cot_ref, act_ref, mem_ref, cot_all, act_all, act_mine,
    gate_ref, seed_mine, seed_other, seed_all, lhs, act4, left_rows, work, inverse, factor_all,
    local1, core1, x1, xs1, z1, zs1, y1, g1, total1,
    local2, core2, x2, xs2, z2, zs2, y2, g2, total2,
    load_sems, seed_sems, act_sems, ring_sems, sems1, sems2,
):
    x, z, c, y = place()
    barrier = pltpu.get_barrier_semaphore()
    count = 0
    for axis in ("core", "x", "z", "y"):
        for _, device in peers(axis):
            pl.semaphore_signal(barrier, inc=1, device_id=device, device_id_type=MESH)
            count += 1
    parts = [
        (source.at[pl.ds(at, step)], target.at[pl.ds(at, step)])
        for source, target, step in (
            (act_hbm, act_ref, 304), (cot_hbm, cot_ref, 32), (mem_hbm, mem_ref, 24),
        )
        for at in range(0, source.shape[0] // step * step, step)
    ]
    last = pl.ds(ROWS // 24 * 24, ROWS % 24)
    parts.append((mem_hbm.at[last], mem_ref.at[last]))
    loads = [
        pltpu.make_async_copy(source, target, load_sems.at[index])
        for index, (source, target) in enumerate(parts)
    ]
    for load in loads:
        load.start()
    ring = Ring(cot_all, ring_sems)

    high, low = split(seed_ref[...])
    both = jnp.concatenate([high.astype(F32), low.astype(F32)], axis=0)
    packed = both.T.astype(BF16)
    seed_mine[y] = jnp.where(c == 0, packed[0:SEED_PART], packed[SEED_SKIP:COLS])

    act_copies = []

    def prepare():
        for load in loads:
            load.wait()
        cot_all[y] = cot_ref[...]
        act_all[y] = act_ref[window(y), :]
        row = lax.broadcasted_iota(jnp.int32, table_ref.shape, 0)
        gate_ref[...] = jnp.sum(
            jnp.where(row == step_ref[0], table_ref[...], 0.0), axis=0, keepdims=True
        )
        gated_high, gated_low = split(cot_ref[...].astype(F32) * gate_ref[...])
        lhs[0:128, :] = gated_high
        lhs[128:256, :] = gated_low
        mem_high, mem_low = split(mem_ref[...])
        lhs[256 : 256 + ROWS, :] = mem_high
        lhs[416 : 416 + ROWS, :] = mem_low
        top, bottom = act_ref[0:HALF, :], act_ref[HALF:DIN, :]
        act4[:, 0:128] = top
        act4[:, 128:256] = top
        act4[:, 256:384] = bottom
        act4[:, 384:512] = bottom
        xs1[...] = jnp.zeros_like(xs1)
        xs2[...] = jnp.zeros_like(xs2)

    pl.semaphore_wait(barrier, count)
    def first_blocks():
        act_copies.extend(
            start_exchange(
                "y", lambda o: (act_ref.at[window(o)], act_all.at[y]),
                act_sems.at[0], act_sems.at[1],
            )
        )
        ring.send(0)

    def to_sibling(block, index):
        (_, device), = peers("core")
        copy = pltpu.make_async_remote_copy(
            src_ref=seed_mine.at[block],
            dst_ref=seed_other.at[block],
            send_sem=seed_sems.at[0, 1, index],
            recv_sem=seed_sems.at[1, 1, index],
            device_id=device,
            device_id_type=MESH,
        )
        copy.start()
        return copy

    along_y = start_exchange(
        "y", lambda o: (seed_mine.at[y], seed_mine.at[y]),
        seed_sems.at[0, 0], seed_sems.at[1, 0],
    )
    swaps = [to_sibling(y, 0)]
    prepare()
    for step in (1, 7, 2, 6, 3, 5, 4):
        along_y[step - 1].wait()
        swaps.append(to_sibling(lax.rem(y + NY - step, NY), step))
    first_blocks()
    for copy in swaps:
        copy.wait()
    for block in range(NY):
        mine, other = seed_mine[block], seed_other[block]
        start = block * COLS
        seed_all[start : start + SEED_PART, :] = jnp.where(c == 0, mine, other)
        seed_all[start + SEED_PART : start + COLS, :] = jnp.where(
            c == 0, other, mine
        )[SEED_PART - SEED_SKIP : SEED_PART]

    product = mm(lhs[...], seed_all[...])
    tokens = product[0:128] + product[128:256]
    tokens = tokens[:, 0:RANK] + tokens[:, RANK:128]
    memory = product[256 : 256 + ROWS] + product[416 : 416 + ROWS]
    memory = memory[:, 0:RANK] + memory[:, RANK:128]
    tok_high, tok_low = split(tokens)
    column = jnp.concatenate([tok_high, tok_low], axis=0)
    blank = jnp.zeros_like(column)
    weights = jnp.concatenate(
        [
            jnp.concatenate([column, blank], axis=1),
            jnp.concatenate([blank, column], axis=1),
        ],
        axis=0,
    )
    local1[0:HALF, :] = mm(act4[...], weights)
    local1[HALF:640, :] = jnp.zeros((640 - HALF, 128), F32)
    my_rows = pl.ds(pl.multiple_of(lax.rem(y, 4) * ROWS, 8), ROWS)
    lane_half = lax.broadcasted_iota(jnp.int32, (ROWS, 128), 1) // RANK
    twice = jnp.concatenate([memory, memory], axis=1)
    local1[my_rows, :] = local1[my_rows, :] + jnp.where(lane_half == y // 4, twice, 0.0)

    def later_blocks():
        ring.send(1)
        ring.pass_on(0)

    sum_everywhere(
        LEFT_PLAN, local1, (core1, x1, xs1, z1, zs1, y1, g1, total1), sems1,
        [None, None, None, later_blocks, None, lambda: ring.pass_on(1), None],
    )

    left_high, left_low = split(total1[0:HALF, :])
    left_rows[0:HALF, :] = jnp.concatenate(
        [left_high[:, 0:RANK], left_low[:, 0:RANK]], axis=1
    )
    left_rows[HALF:DIN, :] = jnp.concatenate(
        [left_high[:, RANK:128], left_low[:, RANK:128]], axis=1
    )
    through = mm(left_rows[...], act_ref[...], ((0,), (0,)))
    through = through[0:RANK] + through[RANK:128]
    thr_high, thr_low = split(through)
    thr_both = jnp.concatenate([thr_high, thr_low], axis=0)
    pair = total1[my_rows, :]
    left_mine = jnp.where(y // 4 == 0, pair[:, 0:RANK], pair[:, RANK:128])
    mine_high, mine_low = split(left_mine)
    mine_both = jnp.concatenate([mine_high, mine_low], axis=1)
    for cols in CHUNKS:
        first, last = cols.start // 128, cols.stop // 128
        by_token = mm(thr_both, cot_ref[:, cols])
        by_high = mm(mine_both, lhs[256 : 256 + ROWS, cols], ((0,), (0,)))
        by_low = mm(mine_high, lhs[416 : 416 + ROWS, cols], ((0,), (0,)))
        right = (by_token[0:RANK] + by_token[RANK:128]) * gate_ref[:, cols]
        right = right + (by_high[0:RANK] + by_high[RANK:128]) + by_low
        for tile in range(first, last):
            at = (tile - first) * 128
            local2[tile * RANK : (tile + 1) * RANK, :] = right[:, at : at + 128]

    def gram():
        grams = mm(left_rows[...], left_rows[...], ((0,), (0,)))
        grams = grams[0:RANK] + grams[RANK:128]
        grams = grams[:, 0:RANK] + grams[:, RANK:128]
        row = lax.broadcasted_iota(jnp.int32, (RANK, RANK), 0)
        col = lax.broadcasted_iota(jnp.int32, (RANK, RANK), 1)
        work[...] = jnp.concatenate([grams, jnp.where(row == col, 1.0, 0.0)], axis=1)

    def eliminate(first, last):
        def step(k, carry):
            row = lax.broadcasted_iota(jnp.int32, (RANK, 128), 0)
            lane = lax.broadcasted_iota(jnp.int32, (RANK, 128), 1)
            whole = work[...]
            pivot_row = work[pl.ds(k, 1), :]
            column = jnp.sum(jnp.where(lane == k, whole, 0.0), axis=1, keepdims=True)
            pivot = jnp.sum(
                jnp.where(lane[0:1] == k, pivot_row, 0.0), axis=1, keepdims=True
            )
            ratio = jnp.where(row[:, 0:1] > k, column / pivot, 0.0)
            work[...] = whole - ratio * pivot_row
            return carry

        lax.fori_loop(first, last, step, 0)

    def finish():
        whole = work[...]
        row = lax.broadcasted_iota(jnp.int32, (RANK, 128), 0)
        lane = lax.broadcasted_iota(jnp.int32, (RANK, 128), 1)
        pivots = jnp.sum(jnp.where(row == lane, whole, 0.0), axis=1, keepdims=True)
        inverse[...] = whole[:, RANK:128] / jnp.sqrt(pivots)

    def merge():
        for source in range(NY):
            rows = act_all[source]
            act_mine[:, source * 128 : (source + 1) * 128] = jnp.where(
                lax.rem(y, 2) == 1, rows[8:SEED_PART], rows[0:ROWS]
            )
        for cols in CHUNKS:
            gradient = mm(act_mine[...], cot_all[:, :, cols].reshape(NY * 128, -1))
            error_ref[:, cols] = gradient * gate_ref[:, cols] + mem_ref[:, cols]

    def core_stage():
        ring.pass_on(2)
        gram()

    def y_stage():
        ring.pass_on(3)
        ring.pass_on(4)
        eliminate(32, 64)

    def last_stage():
        for copy in act_copies:
            copy.wait()
        ring.receive(5)
        ring.receive(6)
        merge()

    sum_everywhere(
        RIGHT_PLAN, local2, (core2, x2, xs2, z2, zs2, y2, g2, total2), sems2,
        [
            core_stage,
            lambda: eliminate(0, 16),
            lambda: eliminate(16, 32),
            y_stage,
            finish,
            None,
            last_stage,
        ],
    )

    inv = inverse[...]
    inv_high, inv_low = split(inv)
    inv_lhs = jnp.concatenate(
        [inv_high.astype(F32), inv_high.astype(F32), inv_low.astype(F32)], axis=1
    ).astype(BF16)
    ortho = lax.dot_general(
        left_mine, inv, (((1,), (1,)), ((), ())),
        precision=lax.Precision.HIGHEST, preferred_element_type=F32,
    )
    ort_high, ort_low = split(ortho)
    ortho_ref[...] = jnp.concatenate(
        [ort_high.astype(F32), ort_high.astype(F32), ort_low.astype(F32)], axis=1
    ).astype(BF16)
    for cols in CHUNKS:
        summed = jnp.concatenate(
            [
                total2[tile * RANK : (tile + 1) * RANK, :]
                for tile in range(cols.start // 128, cols.stop // 128)
            ],
            axis=1,
        )
        high, low = split(summed)
        factor = mm(inv_lhs, jnp.concatenate([high, low, high], axis=0)) * (1.0 / 64)
        factor_all[:, cols] = factor
        high, low = split(factor)
        parts_ref[:, cols] = jnp.concatenate([high, low, high], axis=0)
    mine = jnp.zeros((RANK, COLS), F32)
    for block in range(NY):
        part = factor_all[:, block * COLS : (block + 1) * COLS]
        mine = jnp.where(y == block, part, mine)
    factor_ref[...] = mine
    ring.finish()


def plan_scratch(plan):
    half_rows, x_rows, z_rows = plan
    return [
        pltpu.VMEM((2 * half_rows, 128), F32),
        pltpu.VMEM((half_rows, 128), F32),
        pltpu.VMEM((NX, x_rows, 128), F32),
        pltpu.VMEM((NZ * z_rows, 128), F32),
        pltpu.VMEM((NZ, z_rows, 128), F32),
        pltpu.VMEM((z_rows, 128), F32),
        pltpu.VMEM((NY, z_rows, 128), F32),
        pltpu.VMEM((NC, NX, NZ, z_rows, 128), F32),
        pltpu.VMEM((2 * half_rows, 128), F32),
    ]


def factors(timesteps, gate_table, cot, act_t, memory, seed_t):
    vmem = pl.BlockSpec(memory_space=pltpu.VMEM)
    return pl.pallas_call(
        kernel,
        out_shape=(
            pltpu.VMEM((ROWS, DOUT), F32),
            pltpu.VMEM((ROWS, 3 * RANK), BF16),
            pltpu.VMEM((3 * RANK, DOUT), BF16),
            pltpu.VMEM((RANK, COLS), F32),
        ),
        in_specs=[pl.BlockSpec(memory_space=pltpu.SMEM), vmem]
        + [pl.BlockSpec(memory_space=pltpu.HBM)] * 3
        + [vmem],
        out_specs=(vmem,) * 4,
        scratch_shapes=[
            pltpu.VMEM((128, DOUT), BF16),
            pltpu.VMEM((DIN, 128), BF16),
            pltpu.VMEM((ROWS, DOUT), F32),
            pltpu.VMEM((NY, 128, DOUT), BF16),
            pltpu.VMEM((NY, SEED_PART, 128), BF16),
            pltpu.VMEM((ROWS, NY * 128), BF16),
            pltpu.VMEM((1, DOUT), F32),
            pltpu.VMEM((NY, SEED_PART, 128), BF16),
            pltpu.VMEM((NY, SEED_PART, 128), BF16),
            pltpu.VMEM((DOUT, 128), BF16),
            pltpu.VMEM((576, DOUT), BF16),
            pltpu.VMEM((HALF, 512), BF16),
            pltpu.VMEM((DIN, 128), BF16),
            pltpu.VMEM((RANK, 128), F32),
            pltpu.VMEM((RANK, RANK), F32),
            pltpu.VMEM((RANK, DOUT), F32),
        ]
        + plan_scratch(LEFT_PLAN)
        + plan_scratch(RIGHT_PLAN)
        + [
            pltpu.SemaphoreType.DMA((16,)),
            pltpu.SemaphoreType.DMA((2, 2, 8)),
            pltpu.SemaphoreType.DMA((2, 7)),
            pltpu.SemaphoreType.DMA((2, 2, 7)),
            pltpu.SemaphoreType.DMA((2, 9, 8)),
            pltpu.SemaphoreType.DMA((2, 9, 8)),
        ],
        compiler_params=pltpu.CompilerParams(
            collective_id=0, has_side_effects=True, vmem_limit_bytes=60 * 2**20
        ),
    )(timesteps, gate_table, cot, act_t, memory, seed_t)


def store_kernel(
    merged_ref, ortho_ref, parts_ref, factor_ref, error_out, factor_out, error_ref, sems
):
    copies = [pltpu.make_async_copy(factor_ref, factor_out, sems.at[0])]
    copies[0].start()
    for index, cols in enumerate(CHUNKS):
        error_ref[:, cols] = merged_ref[:, cols] - mm(ortho_ref[...], parts_ref[:, cols])
        copies.append(
            pltpu.make_async_copy(
                error_ref.at[:, cols], error_out.at[:, cols], sems.at[index + 1]
            )
        )
        copies[-1].start()
    for copy in copies:
        copy.wait()


def store(merged, ortho, parts, factor):
    return pl.pallas_call(
        store_kernel,
        out_shape=(
            jax.ShapeDtypeStruct(merged.shape, F32),
            jax.ShapeDtypeStruct(factor.shape, F32),
        ),
        in_specs=[pl.BlockSpec(memory_space=pltpu.VMEM)] * 4,
        out_specs=(pl.BlockSpec(memory_space=pltpu.HBM),) * 2,
        scratch_shapes=[
            pltpu.VMEM((ROWS, DOUT), F32),
            pltpu.SemaphoreType.DMA((1 + len(CHUNKS),)),
        ],
        compiler_params=pltpu.CompilerParams(vmem_limit_bytes=16 * 2**20),
    )(merged, ortho, parts, factor)


def per_device(activations, cotangent, timesteps, gate_table, error_in, seed_factor):
    error_out, factor_t = store(
        *factors(
            timesteps, gate_table, cotangent[0], activations[0].T, error_in[0], seed_factor.T
        )
    )
    return error_out[None], factor_t.T


def solution(mesh):
    placed = (
        P("dp", "seq", None),
        P("dp", "seq", None),
        P("dp"),
        P(),
        P("dp", "seq", None),
        P("seq", None),
    )
    return jax.shard_map(
        per_device,
        mesh=mesh,
        in_specs=placed,
        out_specs=(P("dp", "seq", None), P("seq", None)),
        check_vma=False,
    )
```

```python
import functools

import jax
import jax.numpy as jnp
from jax import lax
from jax.experimental import pallas as pl
from jax.experimental.pallas import tpu as pltpu
from jax.sharding import PartitionSpec as P

MESH = pl.DeviceIdType.MESH
F32 = jnp.float32
BF16 = jnp.bfloat16
NX, NZ, NC, NY = 4, 8, 2, 8
RANK = 64
DIN, DOUT = 1216, 2432
ROWS = DIN // NY
COLS = DOUT // NY
HALF = DIN // 2
SEED_PART = 160
SEED_SKIP = COLS - SEED_PART

LEFT_PLAN = (320, 80, 16)
RIGHT_PLAN = (608, 152, 24)
CHUNKS = tuple(slice(at, min(at + 512, DOUT)) for at in range(0, DOUT, 512))


def split(value):
    high = value.astype(BF16)
    return high, (value - high.astype(F32)).astype(BF16)


def mm(first, second, dims=((1,), (0,))):
    return lax.dot_general(first, second, (dims, ((), ())), preferred_element_type=F32)


def place():
    replica = lax.axis_index("dp")
    return replica // (NZ * NC), (replica // NC) % NZ, replica % NC, lax.axis_index("seq")


def peers(axis):
    x, z, c, y = place()
    count = {"x": NX, "z": NZ, "core": NC, "y": NY}[axis]
    for step in range(1, count):
        if axis == "x":
            other = lax.rem(x + step, NX)
            yield other, (other * (NZ * NC) + z * NC + c, y)
        elif axis == "z":
            other = lax.rem(z + step, NZ)
            yield other, (x * (NZ * NC) + other * NC + c, y)
        elif axis == "core":
            other = 1 - c
            yield other, (x * (NZ * NC) + z * NC + other, y)
        else:
            other = lax.rem(y + step, NY)
            yield other, (x * (NZ * NC) + z * NC + c, other)


def start_exchange(axis, make, send_sems, recv_sems):
    copies = []
    for index, (other, device) in enumerate(peers(axis)):
        source, target = make(other)
        copy = pltpu.make_async_remote_copy(
            src_ref=source,
            dst_ref=target,
            send_sem=send_sems.at[index],
            recv_sem=recv_sems.at[index],
            device_id=device,
            device_id_type=MESH,
        )
        copy.start()
        copies.append(copy)
    return copies


def exchange(axis, make, send_sems, recv_sems, during=None):
    copies = start_exchange(axis, make, send_sems, recv_sems)
    if during is not None:
        during()
    for copy in copies:
        copy.wait()


class Ring:
    def __init__(self, blocks, sems):
        self.blocks, self.sems = blocks, sems
        x, z, c, y = place()
        self.y = y
        line = x * (NZ * NC) + z * NC + c
        self.device = ((line, lax.rem(y + 1, NY)), (line, lax.rem(y + NY - 1, NY)))
        self.sent = []

    def piece(self, way, steps_back, index):
        origin = self.y + (NY - steps_back if way == 0 else steps_back)
        half = index % 2 if way == 0 else 1 - index % 2
        return self.blocks.at[lax.rem(origin, NY), pl.ds(half * 64, 64)]

    def copy(self, way, index, piece):
        return pltpu.make_async_remote_copy(
            src_ref=piece,
            dst_ref=piece,
            send_sem=self.sems.at[0, way, index],
            recv_sem=self.sems.at[1, way, index],
            device_id=self.device[way],
            device_id_type=MESH,
        )

    def send(self, index):
        for way in range(2):
            copy = self.copy(way, index, self.piece(way, index // 2, index))
            copy.start()
            self.sent.append(copy)

    def receive(self, index):
        for way in range(2):
            self.copy(way, index, self.piece(way, index // 2 + 1, index)).wait_recv()

    def pass_on(self, index):
        self.receive(index)
        self.send(index + 2)

    def finish(self):
        for copy in self.sent:
            copy.wait_send()


def window(place_on_y):
    return pl.ds(pl.multiple_of(place_on_y * ROWS // 16 * 16, 16), SEED_PART)


def sum_everywhere(plan, local, bufs, sems, during):
    half_rows, x_rows, z_rows = plan
    used = -(-x_rows // z_rows)
    from_core, from_x, x_sum, from_z, z_sum, from_y, gathered, total = bufs
    x, z, c, y = place()
    (_, sibling), = peers("core")
    x_peers, z_peers = list(peers("x")), list(peers("z"))

    def part(index, rows):
        return pl.ds(pl.multiple_of(index * rows, 8), rows)

    def remote(stage, index, source, target, device):
        return pltpu.make_async_remote_copy(
            src_ref=source,
            dst_ref=target,
            send_sem=sems.at[0, stage, index],
            recv_sem=sems.at[1, stage, index],
            device_id=device,
            device_id_type=MESH,
        )

    def beside(stage):
        if during[stage] is not None:
            during[stage]()

    places = [other for other, _ in x_peers] + [x]
    copies = []
    for index, other in enumerate(places):
        mine = part((1 - c) * NX + other, x_rows)
        copies.append(
            remote(0, index, local.at[mine], from_core.at[part(other, x_rows)], sibling)
        )
        copies[-1].start()
    beside(0)
    x_copies = []
    for index, other in enumerate(places):
        copies[index].wait()
        rows = part(other, x_rows)
        both = local[part(c * NX + other, x_rows), :] + from_core[rows, :]
        if index < NX - 1:
            from_core[rows, :] = both
            x_copies.append(
                remote(1, index, from_core.at[rows], from_x.at[x], x_peers[index][1])
            )
            x_copies[-1].start()
        else:
            from_x[x] = both
    beside(1)
    for copy in x_copies:
        copy.wait()
    x_sum[0:x_rows, :] = (from_x[0] + from_x[1]) + (from_x[2] + from_x[3])

    copies = start_exchange(
        "z", lambda o: (x_sum.at[part(o, z_rows)], from_z.at[z]), sems.at[0, 2], sems.at[1, 2]
    )
    from_z[z] = x_sum[part(z, z_rows), :]
    beside(2)
    for copy in copies:
        copy.wait()
    z_sum[...] = jnp.sum(from_z[...], axis=0)

    copies = start_exchange("y", lambda o: (z_sum, from_y.at[y]), sems.at[0, 3], sems.at[1, 3])
    from_y[y] = z_sum[...]
    beside(3)
    for copy in copies:
        copy.wait()
    gathered[c, x, z] = jnp.sum(from_y[...], axis=0)

    def forward(step):
        piece = lax.rem(z + NZ - step, NZ)
        ref = gathered.at[c, x, piece]
        return piece < used, [
            remote(5 + index, piece, ref, ref, device)
            for index, (_, device) in enumerate(x_peers)
        ]

    def start_forward(step):
        wanted, forwards = forward(step)

        @pl.when(wanted)
        def _():
            for copy in forwards:
                copy.start()

    own = gathered.at[c, x, z]
    copies = start_exchange("z", lambda o: (own, own), sems.at[0, 4], sems.at[1, 4])
    start_forward(0)
    beside(4)
    for step in (1, 7, 2, 6, 3, 5, 4):
        copies[step - 1].wait()
        start_forward(step)

    def to_sibling(index, other):
        ref = gathered.at[c, other, pl.ds(0, used)]
        copy = remote(8, index, ref, ref, sibling)
        copy.start()
        return copy

    copies = [to_sibling(0, x)]
    beside(5)
    for index in (0, 2, 1):
        other = lax.rem(x + NX - 1 - index, NX)
        for piece in range(used):
            ref = gathered.at[c, other, piece]
            remote(5 + index, piece, ref, ref, x_peers[index][1]).wait_recv()
        copies.append(to_sibling(1 + index, other))
    beside(6)
    for copy in copies:
        copy.wait()
    for step in range(NZ):
        wanted, forwards = forward(step)

        @pl.when(wanted)
        def _():
            for copy in forwards:
                copy.wait_send()

    for core in range(NC):
        for at in range(NX):
            first = (core * NX + at) * x_rows
            total[first : first + x_rows, :] = (
                gathered[core, at].reshape(NZ * z_rows, 128)[0:x_rows]
            )


def kernel(
    step_hbm, table_hbm, cot_hbm, act_hbm, mem_hbm, seed_hbm,
    error_ref, ortho_ref, parts_ref, factor_ref,
    step_ref, table_ref, seed_ref, cot_ref, act_ref, mem_ref, cot_all, act_all, act_mine,
    gate_ref, seed_mine, seed_other, seed_all, lhs, act4, left_rows, work, inverse, factor_all,
    local1, core1, x1, xs1, z1, zs1, y1, g1, total1,
    local2, core2, x2, xs2, z2, zs2, y2, g2, total2,
    load_sems, seed_sems, act_sems, ring_sems, sems1, sems2,
):
    x, z, c, y = place()
    barrier = pltpu.get_barrier_semaphore()
    count = 0
    for axis in ("core", "x", "z", "y"):
        for _, device in peers(axis):
            pl.semaphore_signal(barrier, inc=1, device_id=device, device_id_type=MESH)
            count += 1
    seed_load = pltpu.make_async_copy(seed_hbm, seed_ref, load_sems.at[17])
    seed_load.start()
    parts = [(step_hbm, step_ref), (table_hbm, table_ref)] + [
        (source.at[pl.ds(at, step)], target.at[pl.ds(at, step)])
        for source, target, step in (
            (act_hbm, act_ref, 304), (cot_hbm, cot_ref, 32), (mem_hbm, mem_ref, 24),
        )
        for at in range(0, source.shape[0] // step * step, step)
    ]
    last = pl.ds(ROWS // 24 * 24, ROWS % 24)
    parts.append((mem_hbm.at[last], mem_ref.at[last]))
    loads = [
        pltpu.make_async_copy(source, target, load_sems.at[index])
        for index, (source, target) in enumerate(parts)
    ]
    for load in loads:
        load.start()
    ring = Ring(cot_all, ring_sems)

    seed_load.wait()
    high, low = split(seed_ref[...])
    both = jnp.concatenate([high.astype(F32), low.astype(F32)], axis=0)
    packed = both.T.astype(BF16)
    seed_mine[y] = jnp.where(c == 0, packed[0:SEED_PART], packed[SEED_SKIP:COLS])

    act_copies = []

    def prepare():
        for load in loads:
            load.wait()
        cot_all[y] = cot_ref[...]
        act_all[y] = act_ref[window(y), :]
        row = lax.broadcasted_iota(jnp.int32, table_ref.shape, 0)
        gate_ref[...] = jnp.sum(
            jnp.where(row == step_ref[0], table_ref[...], 0.0), axis=0, keepdims=True
        )
        gated_high, gated_low = split(cot_ref[...].astype(F32) * gate_ref[...])
        lhs[0:128, :] = gated_high
        lhs[128:256, :] = gated_low
        mem_high, mem_low = split(mem_ref[...])
        lhs[256 : 256 + ROWS, :] = mem_high
        lhs[416 : 416 + ROWS, :] = mem_low
        top, bottom = act_ref[0:HALF, :], act_ref[HALF:DIN, :]
        act4[:, 0:128] = top
        act4[:, 128:256] = top
        act4[:, 256:384] = bottom
        act4[:, 384:512] = bottom
        xs1[...] = jnp.zeros_like(xs1)
        xs2[...] = jnp.zeros_like(xs2)

    pl.semaphore_wait(barrier, count)
    def first_blocks():
        ring.send(0)
        act_copies.extend(
            start_exchange(
                "y", lambda o: (act_ref.at[window(o)], act_all.at[y]),
                act_sems.at[0], act_sems.at[1],
            )
        )

    def to_sibling(block, index):
        (_, device), = peers("core")
        copy = pltpu.make_async_remote_copy(
            src_ref=seed_mine.at[block],
            dst_ref=seed_other.at[block],
            send_sem=seed_sems.at[0, 1, index],
            recv_sem=seed_sems.at[1, 1, index],
            device_id=device,
            device_id_type=MESH,
        )
        copy.start()
        return copy

    along_y = start_exchange(
        "y", lambda o: (seed_mine.at[y], seed_mine.at[y]),
        seed_sems.at[0, 0], seed_sems.at[1, 0],
    )
    swaps = [to_sibling(y, 0)]
    prepare()
    for step in (1, 7, 2, 6, 3, 5, 4):
        along_y[step - 1].wait()
        swaps.append(to_sibling(lax.rem(y + NY - step, NY), step))
    first_blocks()
    for copy in swaps:
        copy.wait()
    for block in range(NY):
        mine, other = seed_mine[block], seed_other[block]
        start = block * COLS
        seed_all[start : start + SEED_PART, :] = jnp.where(c == 0, mine, other)
        seed_all[start + SEED_PART : start + COLS, :] = jnp.where(
            c == 0, other, mine
        )[SEED_PART - SEED_SKIP : SEED_PART]

    product = mm(lhs[...], seed_all[...])
    tokens = product[0:128] + product[128:256]
    tokens = tokens[:, 0:RANK] + tokens[:, RANK:128]
    memory = product[256 : 256 + ROWS] + product[416 : 416 + ROWS]
    memory = memory[:, 0:RANK] + memory[:, RANK:128]
    tok_high, tok_low = split(tokens)
    column = jnp.concatenate([tok_high, tok_low], axis=0)
    blank = jnp.zeros_like(column)
    weights = jnp.concatenate(
        [
            jnp.concatenate([column, blank], axis=1),
            jnp.concatenate([blank, column], axis=1),
        ],
        axis=0,
    )
    local1[0:HALF, :] = mm(act4[...], weights)
    local1[HALF:640, :] = jnp.zeros((640 - HALF, 128), F32)
    my_rows = pl.ds(pl.multiple_of(lax.rem(y, 4) * ROWS, 8), ROWS)
    lane_half = lax.broadcasted_iota(jnp.int32, (ROWS, 128), 1) // RANK
    twice = jnp.concatenate([memory, memory], axis=1)
    local1[my_rows, :] = local1[my_rows, :] + jnp.where(lane_half == y // 4, twice, 0.0)

    def later_blocks():
        ring.send(1)
        ring.pass_on(0)

    sum_everywhere(
        LEFT_PLAN, local1, (core1, x1, xs1, z1, zs1, y1, g1, total1), sems1,
        [None, None, None, later_blocks, None, lambda: ring.pass_on(1), None],
    )

    left_high, left_low = split(total1[0:HALF, :])
    left_rows[0:HALF, :] = jnp.concatenate(
        [left_high[:, 0:RANK], left_low[:, 0:RANK]], axis=1
    )
    left_rows[HALF:DIN, :] = jnp.concatenate(
        [left_high[:, RANK:128], left_low[:, RANK:128]], axis=1
    )
    through = mm(left_rows[...], act_ref[...], ((0,), (0,)))
    through = through[0:RANK] + through[RANK:128]
    thr_high, thr_low = split(through)
    thr_both = jnp.concatenate([thr_high, thr_low], axis=0)
    pair = total1[my_rows, :]
    left_mine = jnp.where(y // 4 == 0, pair[:, 0:RANK], pair[:, RANK:128])
    mine_high, mine_low = split(left_mine)
    mine_both = jnp.concatenate([mine_high, mine_low], axis=1)
    for cols in CHUNKS:
        first, last = cols.start // 128, cols.stop // 128
        by_token = mm(thr_both, cot_ref[:, cols])
        by_high = mm(mine_both, lhs[256 : 256 + ROWS, cols], ((0,), (0,)))
        by_low = mm(mine_high, lhs[416 : 416 + ROWS, cols], ((0,), (0,)))
        right = (by_token[0:RANK] + by_token[RANK:128]) * gate_ref[:, cols]
        right = right + (by_high[0:RANK] + by_high[RANK:128]) + by_low
        for tile in range(first, last):
            at = (tile - first) * 128
            local2[tile * RANK : (tile + 1) * RANK, :] = right[:, at : at + 128]

    def gram():
        grams = mm(left_rows[...], left_rows[...], ((0,), (0,)))
        grams = grams[0:RANK] + grams[RANK:128]
        grams = grams[:, 0:RANK] + grams[:, RANK:128]
        row = lax.broadcasted_iota(jnp.int32, (RANK, RANK), 0)
        col = lax.broadcasted_iota(jnp.int32, (RANK, RANK), 1)
        work[...] = jnp.concatenate([grams, jnp.where(row == col, 1.0, 0.0)], axis=1)

    def eliminate(first, last):
        def step(k, carry):
            row = lax.broadcasted_iota(jnp.int32, (RANK, 128), 0)
            lane = lax.broadcasted_iota(jnp.int32, (RANK, 128), 1)
            whole = work[...]
            pivot_row = work[pl.ds(k, 1), :]
            column = jnp.sum(jnp.where(lane == k, whole, 0.0), axis=1, keepdims=True)
            pivot = jnp.sum(
                jnp.where(lane[0:1] == k, pivot_row, 0.0), axis=1, keepdims=True
            )
            ratio = jnp.where(row[:, 0:1] > k, column / pivot, 0.0)
            work[...] = whole - ratio * pivot_row
            return carry

        lax.fori_loop(first, last, step, 0)

    def finish():
        whole = work[...]
        row = lax.broadcasted_iota(jnp.int32, (RANK, 128), 0)
        lane = lax.broadcasted_iota(jnp.int32, (RANK, 128), 1)
        pivots = jnp.sum(jnp.where(row == lane, whole, 0.0), axis=1, keepdims=True)
        inverse[...] = whole[:, RANK:128] / jnp.sqrt(pivots)

    def merge():
        for source in range(NY):
            rows = act_all[source]
            act_mine[:, source * 128 : (source + 1) * 128] = jnp.where(
                lax.rem(y, 2) == 1, rows[8:SEED_PART], rows[0:ROWS]
            )
        for cols in CHUNKS:
            gradient = mm(act_mine[...], cot_all[:, :, cols].reshape(NY * 128, -1))
            error_ref[:, cols] = gradient * gate_ref[:, cols] + mem_ref[:, cols]

    def core_stage():
        ring.pass_on(2)
        gram()

    def y_stage():
        ring.pass_on(3)
        ring.pass_on(4)
        eliminate(32, 64)

    def last_stage():
        for copy in act_copies:
            copy.wait()
        ring.receive(5)
        ring.receive(6)
        merge()

    sum_everywhere(
        RIGHT_PLAN, local2, (core2, x2, xs2, z2, zs2, y2, g2, total2), sems2,
        [
            core_stage,
            lambda: eliminate(0, 16),
            lambda: eliminate(16, 32),
            y_stage,
            finish,
            None,
            last_stage,
        ],
    )

    inv = inverse[...]
    inv_high, inv_low = split(inv)
    inv_lhs = jnp.concatenate(
        [inv_high.astype(F32), inv_high.astype(F32), inv_low.astype(F32)], axis=1
    ).astype(BF16)
    ortho = lax.dot_general(
        left_mine, inv, (((1,), (1,)), ((), ())),
        precision=lax.Precision.HIGHEST, preferred_element_type=F32,
    )
    ort_high, ort_low = split(ortho)
    ortho_ref[...] = jnp.concatenate(
        [ort_high.astype(F32), ort_high.astype(F32), ort_low.astype(F32)], axis=1
    ).astype(BF16)
    for cols in CHUNKS:
        summed = jnp.concatenate(
            [
                total2[tile * RANK : (tile + 1) * RANK, :]
                for tile in range(cols.start // 128, cols.stop // 128)
            ],
            axis=1,
        )
        high, low = split(summed)
        factor = mm(inv_lhs, jnp.concatenate([high, low, high], axis=0)) * (1.0 / 64)
        factor_all[:, cols] = factor
        high, low = split(factor)
        parts_ref[:, cols] = jnp.concatenate([high, low, high], axis=0)
    mine = jnp.zeros((RANK, COLS), F32)
    for block in range(NY):
        part = factor_all[:, block * COLS : (block + 1) * COLS]
        mine = jnp.where(y == block, part, mine)
    factor_ref[...] = mine
    ring.finish()


def plan_scratch(plan):
    half_rows, x_rows, z_rows = plan
    return [
        pltpu.VMEM((2 * half_rows, 128), F32),
        pltpu.VMEM((half_rows, 128), F32),
        pltpu.VMEM((NX, x_rows, 128), F32),
        pltpu.VMEM((NZ * z_rows, 128), F32),
        pltpu.VMEM((NZ, z_rows, 128), F32),
        pltpu.VMEM((z_rows, 128), F32),
        pltpu.VMEM((NY, z_rows, 128), F32),
        pltpu.VMEM((NC, NX, NZ, z_rows, 128), F32),
        pltpu.VMEM((2 * half_rows, 128), F32),
    ]


def factors(timesteps, gate_table, cot, act_t, memory, seed_t):
    vmem = pl.BlockSpec(memory_space=pltpu.VMEM)
    return pl.pallas_call(
        kernel,
        out_shape=(
            pltpu.VMEM((ROWS, DOUT), F32),
            pltpu.VMEM((ROWS, 3 * RANK), BF16),
            pltpu.VMEM((3 * RANK, DOUT), BF16),
            pltpu.VMEM((RANK, COLS), F32),
        ),
        in_specs=[pl.BlockSpec(memory_space=pltpu.HBM)] * 6,
        out_specs=(vmem,) * 4,
        scratch_shapes=[
            pltpu.SMEM((1,), jnp.int32),
            pltpu.VMEM(gate_table.shape, F32),
            pltpu.VMEM((RANK, COLS), F32),
            pltpu.VMEM((128, DOUT), BF16),
            pltpu.VMEM((DIN, 128), BF16),
            pltpu.VMEM((ROWS, DOUT), F32),
            pltpu.VMEM((NY, 128, DOUT), BF16),
            pltpu.VMEM((NY, SEED_PART, 128), BF16),
            pltpu.VMEM((ROWS, NY * 128), BF16),
            pltpu.VMEM((1, DOUT), F32),
            pltpu.VMEM((NY, SEED_PART, 128), BF16),
            pltpu.VMEM((NY, SEED_PART, 128), BF16),
            pltpu.VMEM((DOUT, 128), BF16),
            pltpu.VMEM((576, DOUT), BF16),
            pltpu.VMEM((HALF, 512), BF16),
            pltpu.VMEM((DIN, 128), BF16),
            pltpu.VMEM((RANK, 128), F32),
            pltpu.VMEM((RANK, RANK), F32),
            pltpu.VMEM((RANK, DOUT), F32),
        ]
        + plan_scratch(LEFT_PLAN)
        + plan_scratch(RIGHT_PLAN)
        + [
            pltpu.SemaphoreType.DMA((18,)),
            pltpu.SemaphoreType.DMA((2, 2, 8)),
            pltpu.SemaphoreType.DMA((2, 7)),
            pltpu.SemaphoreType.DMA((2, 2, 7)),
            pltpu.SemaphoreType.DMA((2, 9, 8)),
            pltpu.SemaphoreType.DMA((2, 9, 8)),
        ],
        compiler_params=pltpu.CompilerParams(
            collective_id=0, has_side_effects=True, vmem_limit_bytes=60 * 2**20
        ),
    )(timesteps, gate_table, cot, act_t, memory, seed_t)


def store_kernel(
    merged_ref, ortho_ref, parts_ref, factor_ref, error_out, factor_out, error_ref, sems
):
    copies = [pltpu.make_async_copy(factor_ref, factor_out, sems.at[0])]
    copies[0].start()
    for index, cols in enumerate(CHUNKS):
        error_ref[:, cols] = merged_ref[:, cols] - mm(ortho_ref[...], parts_ref[:, cols])
        copies.append(
            pltpu.make_async_copy(
                error_ref.at[:, cols], error_out.at[:, cols], sems.at[index + 1]
            )
        )
        copies[-1].start()
    for copy in copies:
        copy.wait()


def store(merged, ortho, parts, factor):
    return pl.pallas_call(
        store_kernel,
        out_shape=(
            jax.ShapeDtypeStruct(merged.shape, F32),
            jax.ShapeDtypeStruct(factor.shape, F32),
        ),
        in_specs=[pl.BlockSpec(memory_space=pltpu.VMEM)] * 4,
        out_specs=(pl.BlockSpec(memory_space=pltpu.HBM),) * 2,
        scratch_shapes=[
            pltpu.VMEM((ROWS, DOUT), F32),
            pltpu.SemaphoreType.DMA((1 + len(CHUNKS),)),
        ],
        compiler_params=pltpu.CompilerParams(vmem_limit_bytes=16 * 2**20),
    )(merged, ortho, parts, factor)


def per_device(activations, cotangent, timesteps, gate_table, error_in, seed_factor):
    error_out, factor_t = store(
        *factors(
            timesteps, gate_table, cotangent[0], activations[0].T, error_in[0], seed_factor.T
        )
    )
    return error_out[None], factor_t.T


def solution(mesh):
    placed = (
        P("dp", "seq", None),
        P("dp", "seq", None),
        P("dp"),
        P(),
        P("dp", "seq", None),
        P("seq", None),
    )
    return jax.shard_map(
        per_device,
        mesh=mesh,
        in_specs=placed,
        out_specs=(P("dp", "seq", None), P("seq", None)),
        check_vma=False,
    )
```

```python
import functools

import jax
import jax.numpy as jnp
from jax import lax
from jax.experimental import pallas as pl
from jax.experimental.pallas import tpu as pltpu
from jax.sharding import PartitionSpec as P

MESH = pl.DeviceIdType.MESH
F32 = jnp.float32
BF16 = jnp.bfloat16
NX, NZ, NC, NY = 4, 8, 2, 8
RANK = 64
DIN, DOUT = 1216, 2432
ROWS = DIN // NY
COLS = DOUT // NY
HALF = DIN // 2
SEED_PART = 160
SEED_SKIP = COLS - SEED_PART

LEFT_PLAN = (320, 80, 16)
RIGHT_PLAN = (608, 152, 24)
CHUNKS = tuple(slice(at, min(at + 512, DOUT)) for at in range(0, DOUT, 512))


def split(value):
    high = value.astype(BF16)
    return high, (value - high.astype(F32)).astype(BF16)


def mm(first, second, dims=((1,), (0,))):
    return lax.dot_general(first, second, (dims, ((), ())), preferred_element_type=F32)


def place():
    replica = lax.axis_index("dp")
    return replica // (NZ * NC), (replica // NC) % NZ, replica % NC, lax.axis_index("seq")


def peers(axis):
    x, z, c, y = place()
    count = {"x": NX, "z": NZ, "core": NC, "y": NY}[axis]
    for step in range(1, count):
        if axis == "x":
            other = lax.rem(x + step, NX)
            yield other, (other * (NZ * NC) + z * NC + c, y)
        elif axis == "z":
            other = lax.rem(z + step, NZ)
            yield other, (x * (NZ * NC) + other * NC + c, y)
        elif axis == "core":
            other = 1 - c
            yield other, (x * (NZ * NC) + z * NC + other, y)
        else:
            other = lax.rem(y + step, NY)
            yield other, (x * (NZ * NC) + z * NC + c, other)


def start_exchange(axis, make, send_sems, recv_sems):
    copies = []
    for index, (other, device) in enumerate(peers(axis)):
        source, target = make(other)
        copy = pltpu.make_async_remote_copy(
            src_ref=source,
            dst_ref=target,
            send_sem=send_sems.at[index],
            recv_sem=recv_sems.at[index],
            device_id=device,
            device_id_type=MESH,
        )
        copies.append(copy)
    middle = (len(copies) - 1) / 2
    for index in sorted(range(len(copies)), key=lambda at: abs(at - middle)):
        copies[index].start()
    return copies


def exchange(axis, make, send_sems, recv_sems, during=None):
    copies = start_exchange(axis, make, send_sems, recv_sems)
    if during is not None:
        during()
    for copy in copies:
        copy.wait()


class Ring:
    def __init__(self, blocks, sems):
        self.blocks, self.sems = blocks, sems
        x, z, c, y = place()
        self.y = y
        line = x * (NZ * NC) + z * NC + c
        self.device = ((line, lax.rem(y + 1, NY)), (line, lax.rem(y + NY - 1, NY)))
        self.sent = []

    def piece(self, way, steps_back, index):
        origin = self.y + (NY - steps_back if way == 0 else steps_back)
        half = index % 2 if way == 0 else 1 - index % 2
        return self.blocks.at[lax.rem(origin, NY), pl.ds(half * 64, 64)]

    def copy(self, way, index, piece):
        return pltpu.make_async_remote_copy(
            src_ref=piece,
            dst_ref=piece,
            send_sem=self.sems.at[0, way, index],
            recv_sem=self.sems.at[1, way, index],
            device_id=self.device[way],
            device_id_type=MESH,
        )

    def send(self, index):
        for way in range(2):
            copy = self.copy(way, index, self.piece(way, index // 2, index))
            copy.start()
            self.sent.append(copy)

    def receive(self, index):
        for way in range(2):
            self.copy(way, index, self.piece(way, index // 2 + 1, index)).wait_recv()

    def pass_on(self, index):
        self.receive(index)
        self.send(index + 2)

    def finish(self):
        for copy in self.sent:
            copy.wait_send()


def window(place_on_y):
    return pl.ds(pl.multiple_of(place_on_y * ROWS // 16 * 16, 16), SEED_PART)


def sum_everywhere(plan, local, bufs, sems, during):
    half_rows, x_rows, z_rows = plan
    used = -(-x_rows // z_rows)
    from_core, from_x, x_sum, from_z, z_sum, from_y, gathered, total = bufs
    x, z, c, y = place()
    (_, sibling), = peers("core")
    x_peers, z_peers = list(peers("x")), list(peers("z"))

    def part(index, rows):
        return pl.ds(pl.multiple_of(index * rows, 8), rows)

    def remote(stage, index, source, target, device):
        return pltpu.make_async_remote_copy(
            src_ref=source,
            dst_ref=target,
            send_sem=sems.at[0, stage, index],
            recv_sem=sems.at[1, stage, index],
            device_id=device,
            device_id_type=MESH,
        )

    def beside(stage):
        if during[stage] is not None:
            during[stage]()

    places = [other for other, _ in x_peers] + [x]
    copies = []
    for index, other in enumerate(places):
        mine = part((1 - c) * NX + other, x_rows)
        copies.append(
            remote(0, index, local.at[mine], from_core.at[part(other, x_rows)], sibling)
        )
        copies[-1].start()
    beside(0)
    x_copies = []
    for index, other in enumerate(places):
        copies[index].wait()
        rows = part(other, x_rows)
        both = local[part(c * NX + other, x_rows), :] + from_core[rows, :]
        if index < NX - 1:
            from_core[rows, :] = both
            x_copies.append(
                remote(1, index, from_core.at[rows], from_x.at[x], x_peers[index][1])
            )
            x_copies[-1].start()
        else:
            from_x[x] = both
    beside(1)
    for copy in x_copies:
        copy.wait()
    x_sum[0:x_rows, :] = (from_x[0] + from_x[1]) + (from_x[2] + from_x[3])

    copies = start_exchange(
        "z", lambda o: (x_sum.at[part(o, z_rows)], from_z.at[z]), sems.at[0, 2], sems.at[1, 2]
    )
    from_z[z] = x_sum[part(z, z_rows), :]
    beside(2)
    for copy in copies:
        copy.wait()
    z_sum[...] = jnp.sum(from_z[...], axis=0)

    copies = start_exchange("y", lambda o: (z_sum, from_y.at[y]), sems.at[0, 3], sems.at[1, 3])
    from_y[y] = z_sum[...]
    beside(3)
    for copy in copies:
        copy.wait()
    gathered[c, x, z] = jnp.sum(from_y[...], axis=0)

    def forward(step):
        piece = lax.rem(z + NZ - step, NZ)
        ref = gathered.at[c, x, piece]
        return piece < used, [
            remote(5 + index, piece, ref, ref, device)
            for index, (_, device) in enumerate(x_peers)
        ]

    def start_forward(step):
        wanted, forwards = forward(step)

        @pl.when(wanted)
        def _():
            for copy in forwards:
                copy.start()

    own = gathered.at[c, x, z]
    copies = start_exchange("z", lambda o: (own, own), sems.at[0, 4], sems.at[1, 4])
    start_forward(0)
    beside(4)
    for step in (1, 7, 2, 6, 3, 5, 4):
        copies[step - 1].wait()
        start_forward(step)

    def to_sibling(index, other):
        ref = gathered.at[c, other, pl.ds(0, used)]
        copy = remote(8, index, ref, ref, sibling)
        copy.start()
        return copy

    copies = [to_sibling(0, x)]
    beside(5)
    for index in (0, 2, 1):
        other = lax.rem(x + NX - 1 - index, NX)
        for piece in range(used):
            ref = gathered.at[c, other, piece]
            remote(5 + index, piece, ref, ref, x_peers[index][1]).wait_recv()
        copies.append(to_sibling(1 + index, other))
    beside(6)
    for copy in copies:
        copy.wait()
    for step in range(NZ):
        wanted, forwards = forward(step)

        @pl.when(wanted)
        def _():
            for copy in forwards:
                copy.wait_send()

    for core in range(NC):
        for at in range(NX):
            first = (core * NX + at) * x_rows
            total[first : first + x_rows, :] = (
                gathered[core, at].reshape(NZ * z_rows, 128)[0:x_rows]
            )


def kernel(
    step_hbm, table_hbm, cot_hbm, act_hbm, mem_hbm, seed_hbm,
    error_ref, ortho_ref, parts_ref, factor_ref,
    step_ref, table_ref, seed_ref, cot_ref, act_ref, mem_ref, cot_all, act_all, act_mine,
    gate_ref, seed_mine, seed_other, seed_all, lhs, act4, left_rows, work, inverse, factor_all,
    local1, core1, x1, xs1, z1, zs1, y1, g1, total1,
    local2, core2, x2, xs2, z2, zs2, y2, g2, total2,
    load_sems, seed_sems, act_sems, ring_sems, sems1, sems2,
):
    x, z, c, y = place()
    barrier = pltpu.get_barrier_semaphore()
    count = 0
    for axis in ("z", "y", "x", "core"):
        for _, device in peers(axis):
            pl.semaphore_signal(barrier, inc=1, device_id=device, device_id_type=MESH)
            count += 1
    seed_load = pltpu.make_async_copy(seed_hbm, seed_ref, load_sems.at[17])
    seed_load.start()
    parts = [(step_hbm, step_ref), (table_hbm, table_ref)] + [
        (source.at[pl.ds(at, step)], target.at[pl.ds(at, step)])
        for source, target, step in (
            (act_hbm, act_ref, 304), (cot_hbm, cot_ref, 32), (mem_hbm, mem_ref, 24),
        )
        for at in range(0, source.shape[0] // step * step, step)
    ]
    last = pl.ds(ROWS // 24 * 24, ROWS % 24)
    parts.append((mem_hbm.at[last], mem_ref.at[last]))
    loads = [
        pltpu.make_async_copy(source, target, load_sems.at[index])
        for index, (source, target) in enumerate(parts)
    ]
    for load in loads:
        load.start()
    ring = Ring(cot_all, ring_sems)

    seed_load.wait()
    high, low = split(seed_ref[...])
    both = jnp.concatenate([high.astype(F32), low.astype(F32)], axis=0)
    packed = both.T.astype(BF16)
    seed_mine[y] = jnp.where(c == 0, packed[0:SEED_PART], packed[SEED_SKIP:COLS])

    act_copies = []

    def prepare():
        for load in loads:
            load.wait()
        cot_all[y] = cot_ref[...]
        act_all[y] = act_ref[window(y), :]
        row = lax.broadcasted_iota(jnp.int32, table_ref.shape, 0)
        gate_ref[...] = jnp.sum(
            jnp.where(row == step_ref[0], table_ref[...], 0.0), axis=0, keepdims=True
        )
        gated_high, gated_low = split(cot_ref[...].astype(F32) * gate_ref[...])
        lhs[0:128, :] = gated_high
        lhs[128:256, :] = gated_low
        mem_high, mem_low = split(mem_ref[...])
        lhs[256 : 256 + ROWS, :] = mem_high
        lhs[416 : 416 + ROWS, :] = mem_low
        top, bottom = act_ref[0:HALF, :], act_ref[HALF:DIN, :]
        act4[:, 0:128] = top
        act4[:, 128:256] = top
        act4[:, 256:384] = bottom
        act4[:, 384:512] = bottom
        xs1[...] = jnp.zeros_like(xs1)
        xs2[...] = jnp.zeros_like(xs2)

    pl.semaphore_wait(barrier, count)
    def first_blocks():
        ring.send(0)
        act_copies.extend(
            start_exchange(
                "y", lambda o: (act_ref.at[window(o)], act_all.at[y]),
                act_sems.at[0], act_sems.at[1],
            )
        )

    def to_sibling(block, index):
        (_, device), = peers("core")
        copy = pltpu.make_async_remote_copy(
            src_ref=seed_mine.at[block],
            dst_ref=seed_other.at[block],
            send_sem=seed_sems.at[0, 1, index],
            recv_sem=seed_sems.at[1, 1, index],
            device_id=device,
            device_id_type=MESH,
        )
        copy.start()
        return copy

    along_y = start_exchange(
        "y", lambda o: (seed_mine.at[y], seed_mine.at[y]),
        seed_sems.at[0, 0], seed_sems.at[1, 0],
    )
    swaps = [to_sibling(y, 0)]
    prepare()
    for step in (1, 7, 2, 6, 3, 5, 4):
        along_y[step - 1].wait()
        swaps.append(to_sibling(lax.rem(y + NY - step, NY), step))
    first_blocks()
    for copy in swaps:
        copy.wait()
    for block in range(NY):
        mine, other = seed_mine[block], seed_other[block]
        start = block * COLS
        seed_all[start : start + SEED_PART, :] = jnp.where(c == 0, mine, other)
        seed_all[start + SEED_PART : start + COLS, :] = jnp.where(
            c == 0, other, mine
        )[SEED_PART - SEED_SKIP : SEED_PART]

    product = mm(lhs[...], seed_all[...])
    tokens = product[0:128] + product[128:256]
    tokens = tokens[:, 0:RANK] + tokens[:, RANK:128]
    memory = product[256 : 256 + ROWS] + product[416 : 416 + ROWS]
    memory = memory[:, 0:RANK] + memory[:, RANK:128]
    tok_high, tok_low = split(tokens)
    column = jnp.concatenate([tok_high, tok_low], axis=0)
    blank = jnp.zeros_like(column)
    weights = jnp.concatenate(
        [
            jnp.concatenate([column, blank], axis=1),
            jnp.concatenate([blank, column], axis=1),
        ],
        axis=0,
    )
    local1[0:HALF, :] = mm(act4[...], weights)
    local1[HALF:640, :] = jnp.zeros((640 - HALF, 128), F32)
    my_rows = pl.ds(pl.multiple_of(lax.rem(y, 4) * ROWS, 8), ROWS)
    lane_half = lax.broadcasted_iota(jnp.int32, (ROWS, 128), 1) // RANK
    twice = jnp.concatenate([memory, memory], axis=1)
    local1[my_rows, :] = local1[my_rows, :] + jnp.where(lane_half == y // 4, twice, 0.0)

    def later_blocks():
        ring.send(1)
        ring.pass_on(0)

    sum_everywhere(
        LEFT_PLAN, local1, (core1, x1, xs1, z1, zs1, y1, g1, total1), sems1,
        [None, None, None, later_blocks, None, lambda: ring.pass_on(1), None],
    )

    left_high, left_low = split(total1[0:HALF, :])
    left_rows[0:HALF, :] = jnp.concatenate(
        [left_high[:, 0:RANK], left_low[:, 0:RANK]], axis=1
    )
    left_rows[HALF:DIN, :] = jnp.concatenate(
        [left_high[:, RANK:128], left_low[:, RANK:128]], axis=1
    )
    through = mm(left_rows[...], act_ref[...], ((0,), (0,)))
    through = through[0:RANK] + through[RANK:128]
    thr_high, thr_low = split(through)
    thr_both = jnp.concatenate([thr_high, thr_low], axis=0)
    pair = total1[my_rows, :]
    left_mine = jnp.where(y // 4 == 0, pair[:, 0:RANK], pair[:, RANK:128])
    mine_high, mine_low = split(left_mine)
    mine_both = jnp.concatenate([mine_high, mine_low], axis=1)
    for cols in CHUNKS:
        first, last = cols.start // 128, cols.stop // 128
        by_token = mm(thr_both, cot_ref[:, cols])
        by_high = mm(mine_both, lhs[256 : 256 + ROWS, cols], ((0,), (0,)))
        by_low = mm(mine_high, lhs[416 : 416 + ROWS, cols], ((0,), (0,)))
        right = (by_token[0:RANK] + by_token[RANK:128]) * gate_ref[:, cols]
        right = right + (by_high[0:RANK] + by_high[RANK:128]) + by_low
        for tile in range(first, last):
            at = (tile - first) * 128
            local2[tile * RANK : (tile + 1) * RANK, :] = right[:, at : at + 128]

    def gram():
        grams = mm(left_rows[...], left_rows[...], ((0,), (0,)))
        grams = grams[0:RANK] + grams[RANK:128]
        grams = grams[:, 0:RANK] + grams[:, RANK:128]
        row = lax.broadcasted_iota(jnp.int32, (RANK, RANK), 0)
        col = lax.broadcasted_iota(jnp.int32, (RANK, RANK), 1)
        work[...] = jnp.concatenate([grams, jnp.where(row == col, 1.0, 0.0)], axis=1)

    def eliminate(first, last):
        def step(k, carry):
            row = lax.broadcasted_iota(jnp.int32, (RANK, 128), 0)
            lane = lax.broadcasted_iota(jnp.int32, (RANK, 128), 1)
            whole = work[...]
            pivot_row = work[pl.ds(k, 1), :]
            column = jnp.sum(jnp.where(lane == k, whole, 0.0), axis=1, keepdims=True)
            pivot = jnp.sum(
                jnp.where(lane[0:1] == k, pivot_row, 0.0), axis=1, keepdims=True
            )
            ratio = jnp.where(row[:, 0:1] > k, column / pivot, 0.0)
            work[...] = whole - ratio * pivot_row
            return carry

        lax.fori_loop(first, last, step, 0)

    def finish():
        whole = work[...]
        row = lax.broadcasted_iota(jnp.int32, (RANK, 128), 0)
        lane = lax.broadcasted_iota(jnp.int32, (RANK, 128), 1)
        pivots = jnp.sum(jnp.where(row == lane, whole, 0.0), axis=1, keepdims=True)
        inverse[...] = whole[:, RANK:128] / jnp.sqrt(pivots)

    def merge():
        for source in range(NY):
            rows = act_all[source]
            act_mine[:, source * 128 : (source + 1) * 128] = jnp.where(
                lax.rem(y, 2) == 1, rows[8:SEED_PART], rows[0:ROWS]
            )
        for cols in CHUNKS:
            gradient = mm(act_mine[...], cot_all[:, :, cols].reshape(NY * 128, -1))
            error_ref[:, cols] = gradient * gate_ref[:, cols] + mem_ref[:, cols]

    def core_stage():
        ring.pass_on(2)
        gram()

    def y_stage():
        ring.pass_on(3)
        ring.pass_on(4)
        eliminate(32, 64)

    def last_stage():
        for copy in act_copies:
            copy.wait()
        ring.receive(5)
        ring.receive(6)
        merge()

    sum_everywhere(
        RIGHT_PLAN, local2, (core2, x2, xs2, z2, zs2, y2, g2, total2), sems2,
        [
            core_stage,
            lambda: eliminate(0, 16),
            lambda: eliminate(16, 32),
            y_stage,
            finish,
            None,
            last_stage,
        ],
    )

    inv = inverse[...]
    inv_high, inv_low = split(inv)
    inv_lhs = jnp.concatenate(
        [inv_high.astype(F32), inv_high.astype(F32), inv_low.astype(F32)], axis=1
    ).astype(BF16)
    ortho = lax.dot_general(
        left_mine, inv, (((1,), (1,)), ((), ())),
        precision=lax.Precision.HIGHEST, preferred_element_type=F32,
    )
    ort_high, ort_low = split(ortho)
    ortho_ref[...] = jnp.concatenate(
        [ort_high.astype(F32), ort_high.astype(F32), ort_low.astype(F32)], axis=1
    ).astype(BF16)
    for cols in CHUNKS:
        summed = jnp.concatenate(
            [
                total2[tile * RANK : (tile + 1) * RANK, :]
                for tile in range(cols.start // 128, cols.stop // 128)
            ],
            axis=1,
        )
        high, low = split(summed)
        factor = mm(inv_lhs, jnp.concatenate([high, low, high], axis=0)) * (1.0 / 64)
        factor_all[:, cols] = factor
        high, low = split(factor)
        parts_ref[:, cols] = jnp.concatenate([high, low, high], axis=0)
    mine = jnp.zeros((RANK, COLS), F32)
    for block in range(NY):
        part = factor_all[:, block * COLS : (block + 1) * COLS]
        mine = jnp.where(y == block, part, mine)
    factor_ref[...] = mine
    ring.finish()


def plan_scratch(plan):
    half_rows, x_rows, z_rows = plan
    return [
        pltpu.VMEM((2 * half_rows, 128), F32),
        pltpu.VMEM((half_rows, 128), F32),
        pltpu.VMEM((NX, x_rows, 128), F32),
        pltpu.VMEM((NZ * z_rows, 128), F32),
        pltpu.VMEM((NZ, z_rows, 128), F32),
        pltpu.VMEM((z_rows, 128), F32),
        pltpu.VMEM((NY, z_rows, 128), F32),
        pltpu.VMEM((NC, NX, NZ, z_rows, 128), F32),
        pltpu.VMEM((2 * half_rows, 128), F32),
    ]


def factors(timesteps, gate_table, cot, act_t, memory, seed_t):
    vmem = pl.BlockSpec(memory_space=pltpu.VMEM)
    return pl.pallas_call(
        kernel,
        out_shape=(
            pltpu.VMEM((ROWS, DOUT), F32),
            pltpu.VMEM((ROWS, 3 * RANK), BF16),
            pltpu.VMEM((3 * RANK, DOUT), BF16),
            pltpu.VMEM((RANK, COLS), F32),
        ),
        in_specs=[pl.BlockSpec(memory_space=pltpu.HBM)] * 6,
        out_specs=(vmem,) * 4,
        scratch_shapes=[
            pltpu.SMEM((1,), jnp.int32),
            pltpu.VMEM(gate_table.shape, F32),
            pltpu.VMEM((RANK, COLS), F32),
            pltpu.VMEM((128, DOUT), BF16),
            pltpu.VMEM((DIN, 128), BF16),
            pltpu.VMEM((ROWS, DOUT), F32),
            pltpu.VMEM((NY, 128, DOUT), BF16),
            pltpu.VMEM((NY, SEED_PART, 128), BF16),
            pltpu.VMEM((ROWS, NY * 128), BF16),
            pltpu.VMEM((1, DOUT), F32),
            pltpu.VMEM((NY, SEED_PART, 128), BF16),
            pltpu.VMEM((NY, SEED_PART, 128), BF16),
            pltpu.VMEM((DOUT, 128), BF16),
            pltpu.VMEM((576, DOUT), BF16),
            pltpu.VMEM((HALF, 512), BF16),
            pltpu.VMEM((DIN, 128), BF16),
            pltpu.VMEM((RANK, 128), F32),
            pltpu.VMEM((RANK, RANK), F32),
            pltpu.VMEM((RANK, DOUT), F32),
        ]
        + plan_scratch(LEFT_PLAN)
        + plan_scratch(RIGHT_PLAN)
        + [
            pltpu.SemaphoreType.DMA((18,)),
            pltpu.SemaphoreType.DMA((2, 2, 8)),
            pltpu.SemaphoreType.DMA((2, 7)),
            pltpu.SemaphoreType.DMA((2, 2, 7)),
            pltpu.SemaphoreType.DMA((2, 9, 8)),
            pltpu.SemaphoreType.DMA((2, 9, 8)),
        ],
        compiler_params=pltpu.CompilerParams(
            collective_id=0, has_side_effects=True, vmem_limit_bytes=60 * 2**20
        ),
    )(timesteps, gate_table, cot, act_t, memory, seed_t)


def store_kernel(
    merged_ref, ortho_ref, parts_ref, factor_ref, error_out, factor_out, error_ref, sems
):
    copies = [pltpu.make_async_copy(factor_ref, factor_out, sems.at[0])]
    copies[0].start()
    for index, cols in enumerate(CHUNKS):
        error_ref[:, cols] = merged_ref[:, cols] - mm(ortho_ref[...], parts_ref[:, cols])
        copies.append(
            pltpu.make_async_copy(
                error_ref.at[:, cols], error_out.at[:, cols], sems.at[index + 1]
            )
        )
        copies[-1].start()
    for copy in copies:
        copy.wait()


def store(merged, ortho, parts, factor):
    return pl.pallas_call(
        store_kernel,
        out_shape=(
            jax.ShapeDtypeStruct(merged.shape, F32),
            jax.ShapeDtypeStruct(factor.shape, F32),
        ),
        in_specs=[pl.BlockSpec(memory_space=pltpu.VMEM)] * 4,
        out_specs=(pl.BlockSpec(memory_space=pltpu.HBM),) * 2,
        scratch_shapes=[
            pltpu.VMEM((ROWS, DOUT), F32),
            pltpu.SemaphoreType.DMA((1 + len(CHUNKS),)),
        ],
        compiler_params=pltpu.CompilerParams(vmem_limit_bytes=16 * 2**20),
    )(merged, ortho, parts, factor)


def per_device(activations, cotangent, timesteps, gate_table, error_in, seed_factor):
    error_out, factor_t = store(
        *factors(
            timesteps, gate_table, cotangent[0], activations[0].T, error_in[0], seed_factor.T
        )
    )
    return error_out[None], factor_t.T


def solution(mesh):
    placed = (
        P("dp", "seq", None),
        P("dp", "seq", None),
        P("dp"),
        P(),
        P("dp", "seq", None),
        P("seq", None),
    )
    return jax.shard_map(
        per_device,
        mesh=mesh,
        in_specs=placed,
        out_specs=(P("dp", "seq", None), P("seq", None)),
        check_vma=False,
    )
```
